256 devices in a mesh: ctx: 64 (over z, y, core), tp: 4 (over x).
Axes of the slice: x: 4, y: 4, z: 8, core: 2. Of those that a mesh axis runs over, the one named last changes fastest.
Arguments:
- activations: bfloat16 [16384, 4096], P('ctx', 'tp'), may hold values from -0.875 to 0.875
- queries: bfloat16 [16384, 2048], P('ctx', 'tp'), may hold values from -7 to 7
- key_tensor: bfloat16 [16384, 512], P('ctx', 'tp'), may hold values from -4 to 4
- value_tensor: bfloat16 [16384, 512], P('ctx', 'tp'), may hold values from -6 to 6
- output_gradient: bfloat16 [16384, 2048], P('ctx', 'tp'), may hold values from -96 to 96
- selection: int32 [32, 3], replicated, may hold values from 0 to 30, as said below
- block_order: int32 [32], replicated, may hold values from 0 to 31, each once
Outputs:
- grad_queries: bfloat16 [16384, 2048], P('ctx', 'tp')
- key_gradient: bfloat16 [16384, 512], P('ctx', 'tp')
- value_gradient: bfloat16 [16384, 512], P('ctx', 'tp')
- grad_key_weight: float32 [4096, 512], P('ctx', 'tp')
- grad_value_weight: float32 [4096, 512], P('ctx', 'tp')
The draws below stay inside these ranges and needn't reach their ends.
Inputs may be any that keep to these rules, and one draw needn't show every extreme that they name: `selection`: row b holds entries of 0 to b; its entries below b are distinct, and an entry equal to b marks an empty slot, which occurs only in rows b < 3. The last row selects block 30. Stored block s, rows s * 512 to (s + 1) * 512 - 1 of every token array, holds sequence block block_order[s].
All inputs are finite; a program needn't handle non-finite values.
Results may differ from the reference program's by a relative error of at most 0.0089.
Values may be sent and summed in bfloat16 or wider, within the bound.
A program may use at most 128 MiB of HBM per device.

```python
import jax
import jax.numpy as jnp
from jax import lax

D = 4096
HEAD_SIZE = 128
QUERY_HEADS = 16
KEY_VALUE_HEADS = 4
BLOCK_TOKENS = 512
PICKED_BLOCKS = 3
SEQUENCE_TOKENS = 16384
SEQUENCE_BLOCKS = 32


def draw_queries(key, part):
    key = jax.random.fold_in(key, 5)
    return jax.random.truncated_normal(key, -4.0, 4.0, (SEQUENCE_TOKENS, QUERY_HEADS * HEAD_SIZE), jnp.float32).astype(jnp.bfloat16)


def draw_key_tensor(key, part):
    key = jax.random.fold_in(key, 7)
    drawn_result = jax.random.truncated_normal(key, -4.0, 4.0, (SEQUENCE_TOKENS, KEY_VALUE_HEADS * HEAD_SIZE), jnp.float32)
    return drawn_result.astype(jnp.bfloat16)


def draw_selection(key, part):
    key = jax.random.fold_in(key, 11)
    flag_key, noise_key = jax.random.split(key)
    favored = (jax.random.randint(flag_key, (SEQUENCE_BLOCKS,), 0, 4) == 0).astype(jnp.int32)
    noise_level = jax.random.randint(noise_key, (SEQUENCE_BLOCKS, SEQUENCE_BLOCKS), 0, 4096)
    candidates = jnp.arange(SEQUENCE_BLOCKS, dtype=jnp.int32)
    ranking = (noise_level + 4096 * favored[None, :]) * SEQUENCE_BLOCKS + candidates[None, :]
    forced = (candidates[:, None] == SEQUENCE_BLOCKS - 1) & (candidates[None, :] == SEQUENCE_BLOCKS - 2)
    ranking = jnp.where(forced, 8192 * SEQUENCE_BLOCKS + candidates[None, :], ranking)
    earlier = candidates[None, :] < candidates[:, None]
    ranking = jnp.where(earlier, ranking, -1 - candidates[None, :])
    picks = lax.top_k(ranking, PICKED_BLOCKS)[1].astype(jnp.int32)
    usable = jnp.take_along_axis(earlier, picks, axis=1)
    return jnp.where(usable, picks, candidates[:, None]).astype(jnp.int32)


def spiked(entries, key, source, target, blocks, factor):
    def block_of(dim):
        return (jnp.arange(entries.shape[dim]) // (entries.shape[dim] // blocks)).reshape((-1,) + (1,) * (entries.ndim - 1 - dim))

    near = jax.random.permutation(key, blocks)[block_of(target)]
    far = (block_of(target) + blocks // 2) % blocks
    return jnp.where((block_of(source) == near) | (block_of(source) == far), factor * entries, entries)


def level_of(stream_key, shape, shards, low, largest):
    def one(axis_at, blocks):
        steps = jax.random.uniform(jax.random.fold_in(jax.random.fold_in(stream_key, 6), axis_at), (blocks,), jnp.float32, low / len(shards), largest / len(shards))
        return jnp.repeat(jnp.exp(steps), shape[axis_at] // blocks).reshape((-1,) + (1,) * (len(shape) - axis_at - 1))

    factor_of = one(*shards[0])
    for cut in shards[1:]:
        factor_of = factor_of * one(*cut)
    return factor_of


def normal_values(own_key, dims, width, limit, shards=(), kind=jnp.bfloat16):
    factor_of = level_of(own_key, dims, shards, -0.22, 0.18) if shards else 1.0
    values = jax.random.normal(own_key, dims, jnp.float32) * width * factor_of
    return jnp.minimum(jnp.maximum(values, -limit), limit).astype(kind)


def noise_with(rng, extent, spread, bound, cuts, heavy, kind=jnp.bfloat16):
    entries = spread * jax.random.normal(rng, extent, jnp.float32)
    if cuts:
        entries = entries * level_of(rng, extent, cuts, -0.22, 0.18)
    return jnp.clip(spiked(entries, jax.random.fold_in(rng, 3), *heavy), -bound, bound).astype(kind)


def setup_inputs(seed: int = 0) -> dict:
    keys = jax.random.split(jax.random.key(seed), 8)
    return {
        "activations": noise_with(keys[0], (SEQUENCE_TOKENS, D), 0.05, 0.875, ((0, 64), (1, 4)), (0, 1, 64, 4.0)),
        "queries": draw_queries(jax.random.fold_in(keys[7], 71), 0),
        "key_tensor": draw_key_tensor(jax.random.fold_in(keys[7], 71), 0),
        "value_tensor": normal_values(keys[3], (SEQUENCE_TOKENS, KEY_VALUE_HEADS * HEAD_SIZE), 1.0, 6.0, ((0, 64), (1, 4))),
        "output_gradient": normal_values(keys[4], (SEQUENCE_TOKENS, QUERY_HEADS * HEAD_SIZE), 16.0, 96.0, ((0, 64), (1, 4))),
        "selection": draw_selection(jax.random.fold_in(keys[7], 71), 0),
        "block_order": jax.random.permutation(keys[6], SEQUENCE_BLOCKS).astype(jnp.int32),
    }


NEG_FILL = -1.0e30


def reference(activations, queries, key_tensor, value_tensor, output_gradient, selection, block_order):
    inverse = jnp.zeros((SEQUENCE_BLOCKS,), jnp.int32).at[block_order].set(jnp.arange(SEQUENCE_BLOCKS, dtype=jnp.int32))
    scale_value = HEAD_SIZE ** -0.5
    query_heads_each = QUERY_HEADS // KEY_VALUE_HEADS
    blocked_queries = queries.reshape(SEQUENCE_BLOCKS, BLOCK_TOKENS, KEY_VALUE_HEADS, query_heads_each, HEAD_SIZE)
    gradient_blocks = output_gradient.reshape(SEQUENCE_BLOCKS, BLOCK_TOKENS, KEY_VALUE_HEADS, query_heads_each, HEAD_SIZE)
    blocked_keys = key_tensor.reshape(SEQUENCE_BLOCKS, BLOCK_TOKENS, KEY_VALUE_HEADS, HEAD_SIZE)
    blocked_values = value_tensor.reshape(SEQUENCE_BLOCKS, BLOCK_TOKENS, KEY_VALUE_HEADS, HEAD_SIZE)
    offsets = jnp.arange(BLOCK_TOKENS, dtype=jnp.int32)
    causal = offsets[None, :] <= offsets[:, None]

    def one_block(slot_index):
        own_block = block_order[slot_index]
        listed = selection[own_block]
        chosen = jnp.concatenate([listed, own_block[None]]).astype(jnp.int32)
        slot_sequence = inverse[chosen].astype(jnp.int32)
        active = jnp.concatenate([listed != own_block, jnp.ones((1,), jnp.bool_)])
        pieces = []
        for entry in range(PICKED_BLOCKS):
            pieces.append(jnp.broadcast_to(active[entry], causal.shape))
        pieces.append(causal)
        allowed = jnp.concatenate(pieces, axis=1)
        key_lines = blocked_keys[slot_sequence].reshape((PICKED_BLOCKS + 1) * BLOCK_TOKENS, KEY_VALUE_HEADS, HEAD_SIZE).astype(jnp.float32)
        value_lines = blocked_values[slot_sequence].reshape((PICKED_BLOCKS + 1) * BLOCK_TOKENS, KEY_VALUE_HEADS, HEAD_SIZE).astype(jnp.float32)
        query_wide = blocked_queries[slot_index].astype(jnp.float32)
        grad_wide = gradient_blocks[slot_index].astype(jnp.float32)
        scores = jnp.einsum("rgpd,lgd->gprl", query_wide, key_lines) * scale_value
        scores = jnp.where(allowed[None, None], scores, NEG_FILL)
        row_peak = jnp.max(scores, axis=-1, keepdims=True)
        exponent = jnp.exp(scores - row_peak)
        weights = exponent / jnp.sum(exponent, axis=-1, keepdims=True)
        weights_low = lax.optimization_barrier(weights.astype(jnp.bfloat16)).astype(jnp.float32)
        output = jnp.einsum("gprl,lgd->rgpd", weights_low, value_lines)
        row_delta = jnp.sum(grad_wide * output, axis=-1).transpose(1, 2, 0)
        grad_probs = jnp.einsum("rgpd,lgd->gprl", grad_wide, value_lines)
        grad_scores = weights * (grad_probs - row_delta[..., None])
        grad_scores = lax.optimization_barrier(grad_scores.astype(jnp.bfloat16)).astype(jnp.float32)
        query_gradient = (jnp.einsum("gprl,lgd->rgpd", grad_scores, key_lines) * scale_value).astype(jnp.bfloat16)
        key_portion = jnp.einsum("gprl,rgpd->lgd", grad_scores, query_wide) * scale_value
        value_portion = jnp.einsum("gprl,rgpd->lgd", weights_low, grad_wide)
        return (query_gradient, key_portion.reshape(PICKED_BLOCKS + 1, BLOCK_TOKENS, KEY_VALUE_HEADS, HEAD_SIZE),
                value_portion.reshape(PICKED_BLOCKS + 1, BLOCK_TOKENS, KEY_VALUE_HEADS, HEAD_SIZE), slot_sequence)

    grad_query_all, key_portions, value_portions, slot_lists = lax.map(one_block, jnp.arange(SEQUENCE_BLOCKS, dtype=jnp.int32))
    flattened_slots = slot_lists.reshape(-1)
    key_grand_sum = jnp.zeros((SEQUENCE_BLOCKS, BLOCK_TOKENS, KEY_VALUE_HEADS, HEAD_SIZE), jnp.float32).at[flattened_slots].add(key_portions.reshape(-1, BLOCK_TOKENS, KEY_VALUE_HEADS, HEAD_SIZE))
    value_grand_sum = jnp.zeros((SEQUENCE_BLOCKS, BLOCK_TOKENS, KEY_VALUE_HEADS, HEAD_SIZE), jnp.float32).at[flattened_slots].add(value_portions.reshape(-1, BLOCK_TOKENS, KEY_VALUE_HEADS, HEAD_SIZE))
    key_gradient = key_grand_sum.reshape(SEQUENCE_TOKENS, KEY_VALUE_HEADS * HEAD_SIZE).astype(jnp.bfloat16)
    value_gradient = value_grand_sum.reshape(SEQUENCE_TOKENS, KEY_VALUE_HEADS * HEAD_SIZE).astype(jnp.bfloat16)
    grad_key_weight = jnp.dot(activations.T, key_gradient, preferred_element_type=jnp.float32)
    grad_value_weight = jnp.dot(activations.T, value_gradient, preferred_element_type=jnp.float32)
    grad_queries = grad_query_all.reshape(SEQUENCE_TOKENS, QUERY_HEADS * HEAD_SIZE)
    return grad_queries, key_gradient, value_gradient, grad_key_weight, grad_value_weight
```

```python
import functools
import math

import jax
import jax.numpy as jnp
from jax import lax
from jax.experimental import pallas as pl
from jax.experimental.pallas import tpu as pltpu
from jax.sharding import PartitionSpec as P

MESH = pl.DeviceIdType.MESH
F32 = jnp.float32
BF16 = jnp.bfloat16

HEAD = 128
BLOCK = 512
HALF = 256
PICKS = 3
CHIPS = 32
ROWS_Y = 4
ROWS_Z = 8
ROWS_X = 4
PIECE = BLOCK // CHIPS
HEADS = 4
QUERIES = HEADS * HALF
SCALE = HEAD**-0.5
EXP_SCALE = SCALE * math.log2(math.e)
LOW = -1e30
HIGH = 1e30

(LOAD, P1, OWN, ACT1, P2, SWAP, ACT3, BACK2, BACK1, HALVES, GATHER, SUMS, LAST) = range(13)
BACK0 = 13
ALONG_X = BACK0 + PICKS + 1
SEMS = ALONG_X + ROWS_X


def rows_dot(left, right):
    return lax.dot_general(left, right, (((1,), (1,)), ((), ())), preferred_element_type=F32)


def plain_dot(left, right):
    return lax.dot_general(left, right, (((1,), (0,)), ((), ())), preferred_element_type=F32)


def kernel(
    table,
    live,
    columns,
    act_in,
    q_in,
    k_in,
    v_in,
    go_in,
    dq_out,
    dkv_out,
    dw_out,
    qd,
    own,
    held,
    picked,
    kv,
    key_t,
    scores,
    gprobs,
    low,
    cross,
    crossed,
    terms,
    landed,
    member,
    sums,
    final,
    own_terms,
    grads,
    all_grads,
    grads_t,
    acts,
    wide,
    wide_in,
    w_send,
    w_rows,
    send,
    recv,
):
    c = lax.axis_index("ctx")
    x = lax.axis_index("tp")
    chip = c // 2
    core = c % 2
    z = chip // ROWS_Y
    y = chip % ROWS_Y
    other = 1 - core
    sibling = c + 1 - 2 * core

    def remote(src, dst, sem, ctx, tp=None):
        return pltpu.make_async_remote_copy(
            src_ref=src,
            dst_ref=dst,
            send_sem=send.at[sem],
            recv_sem=recv.at[sem],
            device_id=(ctx, x if tp is None else tp),
            device_id_type=MESH,
        )

    def local(src, dst, sem):
        return pltpu.make_async_copy(src, dst, recv.at[sem])

    def arrived(ref, sem):
        pltpu.make_async_copy(ref, ref, recv.at[sem]).wait()

    def sent(ref, sem):
        pltpu.make_async_copy(ref, ref, send.at[sem]).wait()

    barrier = pltpu.get_barrier_semaphore()

    def greet(d, carry):
        pl.semaphore_signal(
            barrier, inc=1, device_id=(lax.rem(c + d, 2 * CHIPS), x), device_id_type=MESH
        )
        return carry

    lax.fori_loop(1, 2 * CHIPS, greet, 0)
    for d in range(1, ROWS_X):
        pl.semaphore_signal(
            barrier, inc=1, device_id=(c, lax.rem(x + d, ROWS_X)), device_id_type=MESH
        )

    for h in range(HEADS):
        strip = pl.ds(h * HEAD, HEAD)
        block = pl.ds(h * HALF, HALF)
        local(q_in.at[:, strip], qd.at[0, block], LOAD).start()
        local(go_in.at[:, strip], qd.at[1, block], LOAD).start()

    pl.semaphore_wait(barrier, 2 * CHIPS - 1 + ROWS_X - 1)

    def spread(j, carry):
        rows = pl.ds(pl.multiple_of(j * PIECE, PIECE), PIECE)
        for kind, src in ((0, k_in), (1, v_in)):
            target = (core * (CHIPS // 2) + j) * 2 + kind

            @pl.when(target != c)
            def _():
                remote(src.at[rows], held.at[chip], P1, target).start()

            @pl.when(target == c)
            def _():
                local(src.at[rows], held.at[chip], P1).start()

        return carry

    lax.fori_loop(0, CHIPS // 2, spread, 0)

    my_rows = pl.ds(pl.multiple_of(core * HALF, HALF), HALF)
    for kind, src in ((0, k_in), (1, v_in)):
        remote(src, own.at[kind, my_rows], OWN, sibling).start()
        local(src, own.at[kind, my_rows], OWN).start()

    for d in range(ROWS_Y):
        y_to = lax.rem(y + d, ROWS_Y)
        for s in range(2):
            src = act_in.at[:, pl.ds(pl.multiple_of((y_to + ROWS_Y * s) * HEAD, HEAD), HEAD)]
            dst = acts.at[x, core, y, :, pl.ds(s * HEAD, HEAD)]
            if d == 0:
                local(src, dst, ACT1).start()
            else:
                remote(src, dst, ACT1, (z * ROWS_Y + y_to) * 2 + core).start()

    wanted = columns[...]
    step_rows = 64
    for r in range(0, BLOCK, step_rows):
        row = lax.broadcasted_iota(jnp.int32, (step_rows, CHIPS * PICKS * PIECE), 0) + r
        col = lax.broadcasted_iota(jnp.int32, (step_rows, CHIPS * PICKS * PIECE), 1)
        hit = (row // PIECE == wanted) & (row % PIECE == col % PIECE)
        member[pl.ds(r, step_rows), :] = jnp.where(hit, 1.0, 0.0).astype(BF16)

    arrived(held, P1)

    def serve(d, carry):
        target = lax.rem(chip + d, CHIPS)
        for j in range(PICKS):
            picked[target, j] = held[table[target, j]]

        @pl.when(target != chip)
        def _():
            remote(picked.at[target], kv.at[core, chip], P2, target * 2 + core).start()

        @pl.when(target == chip)
        def _():
            local(picked.at[target], kv.at[core, chip], P2).start()

        return carry

    lax.fori_loop(0, CHIPS, serve, 0)

    arrived(acts.at[x, core], ACT1)
    for d in range(1, ROWS_X):
        x_to = lax.rem(x + d, ROWS_X)
        remote(acts.at[x, core], acts.at[x, core], ALONG_X + d, c, x_to).start()

    arrived(own, OWN)
    arrived(qd, LOAD)

    arrived(kv.at[core], P2)
    remote(kv.at[core], kv.at[core], SWAP, sibling).start()
    arrived(kv.at[other], SWAP)

    def lines(kind, j):
        if j == PICKS:
            return own[kind]
        return kv[kind, :, j].reshape(BLOCK, HEAD)

    for j in range(PICKS + 1):
        key_t[j] = lines(0, j).T

    alive = [live[chip, j] != 0 for j in range(PICKS)]

    def one_head(h, carry):
        block = pl.ds(pl.multiple_of(h * HALF, HALF), HALF)
        strip = pl.ds(pl.multiple_of(h * HEAD, HEAD), HEAD)
        queries = qd[0, block, :]
        grads_out = qd[1, block, :]
        peak = None
        for j in range(PICKS + 1):
            raw = rows_dot(lines(0, j), queries)
            if j == PICKS:
                key_at = lax.broadcasted_iota(jnp.int32, raw.shape, 0)
                query_at = lax.broadcasted_iota(jnp.int32, raw.shape, 1) + core * HALF
                raw = jnp.where(key_at <= query_at, raw, LOW)
            scores[j] = raw
            top = jnp.max(raw, axis=0, keepdims=True)
            if j < PICKS:
                top = jnp.where(alive[j], top, LOW)
            peak = top if peak is None else jnp.maximum(peak, top)
        total = jnp.zeros((1, HALF), F32)
        for j in range(PICKS + 1):
            base = peak if j == PICKS else jnp.where(alive[j], peak, HIGH)
            weights = jnp.exp2((scores[j] - base) * EXP_SCALE)
            scores[j] = weights
            total = total + jnp.sum(weights, axis=0, keepdims=True)
        share = 1.0 / total
        delta = jnp.zeros((1, HALF), F32)
        for j in range(PICKS + 1):
            gp = rows_dot(lines(1, j), grads_out)
            gprobs[j] = gp
            delta = delta + jnp.sum(scores[j] * gp, axis=0, keepdims=True)
        delta = delta * share
        dq = jnp.zeros((HEAD, HALF), F32)
        for j in range(PICKS + 1):
            probs = scores[j] * share
            low[1, j, :, block] = probs.astype(BF16)
            gs = (probs * (gprobs[j] - delta)).astype(BF16)
            low[0, j, :, block] = gs
            dq = dq + plain_dot(key_t[j], gs)
        dq_out[:, strip] = (dq * SCALE).T.astype(BF16)
        return carry

    lax.fori_loop(0, HEADS, one_head, 0)

    mine_scale = jnp.where(core == 0, SCALE, 1.0).astype(F32)
    other_scale = jnp.where(core == 0, 1.0, SCALE).astype(F32)
    for j in range(PICKS + 1):
        cross[j] = (plain_dot(low[other, j], qd[other]) * other_scale).astype(BF16)
        remote(cross.at[j], crossed.at[j], BACK0 + j, sibling).start()
    for j in range(PICKS):
        mine = plain_dot(low[core, j], qd[core]) * mine_scale
        arrived(crossed.at[j], BACK0 + j)
        mine = mine + crossed[j].astype(F32)
        terms[:, j] = mine.astype(BF16).reshape(CHIPS, PIECE, HEAD)

    def give(d, carry):
        target = lax.rem(chip + d, CHIPS)

        @pl.when(target != chip)
        def _():
            remote(terms.at[target], landed.at[chip], BACK2, target * 2 + core).start()

        @pl.when(target == chip)
        def _():
            local(terms.at[target], landed.at[chip], BACK2).start()

        return carry

    lax.fori_loop(0, CHIPS, give, 0)

    mine = plain_dot(low[core, PICKS], qd[core]) * mine_scale
    arrived(crossed.at[PICKS], BACK0 + PICKS)
    own_terms[...] = mine + crossed[PICKS].astype(F32)

    for d in range(1, ROWS_X):
        arrived(acts.at[lax.rem(x + ROWS_X - d, ROWS_X), core], ALONG_X + d)
    remote(acts.at[:, core], acts.at[:, core], ACT3, sibling).start()

    arrived(landed, BACK2)
    summed = plain_dot(member[...], landed[...].reshape(CHIPS * PICKS * PIECE, HEAD))
    sums[...] = summed.astype(BF16).reshape(CHIPS, PIECE, HEAD)

    def give_back(d, carry):
        target = lax.rem(chip + d, CHIPS)

        @pl.when(target != chip)
        def _():
            remote(sums.at[target], final.at[chip], BACK1, target * 2 + core).start()

        @pl.when(target == chip)
        def _():
            local(sums.at[target], final.at[chip], BACK1).start()

        return carry

    lax.fori_loop(0, CHIPS, give_back, 0)
    arrived(final, BACK1)
    grads[...] = (final[...].reshape(BLOCK, HEAD).astype(F32) + own_terms[...]).astype(BF16)

    for d in range(ROWS_Y):
        y_to = lax.rem(y + d, ROWS_Y)
        if d == 0:
            local(grads, all_grads.at[y], GATHER).start()
        else:
            remote(grads, all_grads.at[y], GATHER, (z * ROWS_Y + y_to) * 2 + core).start()
    their_rows = pl.ds(pl.multiple_of(other * HALF, HALF), HALF)
    remote(grads.at[their_rows], dkv_out.at[core], HALVES, sibling).start()
    local(grads.at[my_rows], dkv_out.at[core], HALVES).start()

    arrived(all_grads, GATHER)
    for half in range(2):
        for b in range(ROWS_Y):
            grads_t[:, pl.ds((half * ROWS_Y + b) * HALF, HALF)] = all_grads[
                b, pl.ds(half * HALF, HALF), :
            ].T
    arrived(acts.at[:, other], ACT3)
    for a in range(ROWS_X):
        both = plain_dot(grads_t[...], acts[a].reshape(2 * ROWS_Y * HALF, 2 * HEAD))
        wide[2 * a] = both[:, :HEAD]
        wide[2 * a + 1] = both[:, HEAD:]
        w_send[2 * a] = both[:, :HEAD].astype(BF16)
        w_send[2 * a + 1] = both[:, HEAD:].astype(BF16)
    for d in range(1, ROWS_Z):
        z_to = lax.rem(z + d, ROWS_Z)
        remote(w_send.at[z_to], wide_in.at[d - 1], SUMS, (z_to * ROWS_Y + y) * 2 + core).start()
    arrived(wide_in, SUMS)
    acc = wide[z]
    for d in range(ROWS_Z - 1):
        acc = acc + wide_in[d].astype(F32)
    w_rows[...] = acc.T
    keep = pl.ds(pl.multiple_of(core * (HEAD // 2), HEAD // 2), HEAD // 2)
    pass_on = pl.ds(pl.multiple_of(other * (HEAD // 2), HEAD // 2), HEAD // 2)
    remote(w_rows.at[pass_on], dw_out.at[core], LAST, sibling).start()
    local(w_rows.at[keep], dw_out.at[core], LAST).start()
    arrived(dw_out, LAST)
    arrived(dkv_out, HALVES)

    here = chip // (CHIPS // 2) == core

    @pl.when(here)
    def _():
        sent(held.at[pl.ds(0, CHIPS - 1)], P1)

    @pl.when(jnp.logical_not(here))
    def _():
        sent(held, P1)

    sent(own.at[:, pl.ds(0, HALF)], OWN)
    sent(acts.at[0, 0, pl.ds(0, ROWS_Y - 1)], ACT1)
    sent(kv.at[0, pl.ds(0, CHIPS - 1)], P2)
    sent(kv.at[0], SWAP)
    for d in range(1, ROWS_X):
        sent(acts.at[0, 0], ALONG_X + d)
    sent(acts.at[:, 0], ACT3)
    for j in range(PICKS + 1):
        sent(cross.at[j], BACK0 + j)
    sent(terms.at[pl.ds(0, CHIPS - 1)], BACK2)
    sent(sums.at[pl.ds(0, CHIPS - 1)], BACK1)
    sent(all_grads.at[pl.ds(0, ROWS_Y - 1)], GATHER)
    sent(dkv_out.at[0], HALVES)
    sent(w_send.at[pl.ds(0, ROWS_Z - 1)], SUMS)
    sent(dw_out.at[0], LAST)


def body(activations, queries, key_tensor, value_tensor, output_gradient, selection, block_order):
    blocks = jnp.arange(CHIPS, dtype=jnp.int32)
    holds = block_order[:, None] == blocks[None, :]
    asked = jnp.sum(jnp.where(holds[:, :, None], selection[None], 0), axis=1)
    live = (asked != block_order[:, None]).astype(jnp.int32)
    at = asked[:, :, None] == block_order[None, None, :]
    table = jnp.sum(jnp.where(at, blocks[None, None], 0), axis=2).astype(jnp.int32)
    columns = jnp.broadcast_to(table[:, :, None], (CHIPS, PICKS, PIECE)).reshape(1, -1)

    smem = pl.BlockSpec(memory_space=pltpu.SMEM)
    vmem = pl.BlockSpec(memory_space=pltpu.VMEM)
    anywhere = pl.BlockSpec(memory_space=pl.ANY)
    dq, dkv, dw = pl.pallas_call(
        kernel,
        out_shape=(
            jax.ShapeDtypeStruct((HALF, HEADS * HEAD), BF16),
            jax.ShapeDtypeStruct((2, HALF, HEAD), BF16),
            jax.ShapeDtypeStruct((2, HEAD // 2, HEAD), F32),
        ),
        in_specs=[smem, smem, vmem] + [anywhere] * 5,
        out_specs=[vmem] * 3,
        scratch_shapes=[
            pltpu.VMEM((2, QUERIES, HEAD), BF16),
            pltpu.VMEM((2, BLOCK, HEAD), BF16),
            pltpu.VMEM((CHIPS, PIECE, HEAD), BF16),
            pltpu.VMEM((CHIPS, PICKS, PIECE, HEAD), BF16),
            pltpu.VMEM((2, CHIPS, PICKS, PIECE, HEAD), BF16),
            pltpu.VMEM((PICKS + 1, HEAD, BLOCK), BF16),
            pltpu.VMEM((PICKS + 1, BLOCK, HALF), F32),
            pltpu.VMEM((PICKS + 1, BLOCK, HALF), F32),
            pltpu.VMEM((2, PICKS + 1, BLOCK, QUERIES), BF16),
            pltpu.VMEM((PICKS + 1, BLOCK, HEAD), BF16),
            pltpu.VMEM((PICKS + 1, BLOCK, HEAD), BF16),
            pltpu.VMEM((CHIPS, PICKS, PIECE, HEAD), BF16),
            pltpu.VMEM((CHIPS, PICKS, PIECE, HEAD), BF16),
            pltpu.VMEM((BLOCK, CHIPS * PICKS * PIECE), BF16),
            pltpu.VMEM((CHIPS, PIECE, HEAD), BF16),
            pltpu.VMEM((CHIPS, PIECE, HEAD), BF16),
            pltpu.VMEM((BLOCK, HEAD), F32),
            pltpu.VMEM((BLOCK, HEAD), BF16),
            pltpu.VMEM((ROWS_Y, BLOCK, HEAD), BF16),
            pltpu.VMEM((HEAD, ROWS_Y * BLOCK), BF16),
            pltpu.VMEM((ROWS_X, 2, ROWS_Y, HALF, 2 * HEAD), BF16),
            pltpu.VMEM((ROWS_Z, HEAD, HEAD), F32),
            pltpu.VMEM((ROWS_Z - 1, HEAD, HEAD), BF16),
            pltpu.VMEM((ROWS_Z, HEAD, HEAD), BF16),
            pltpu.VMEM((HEAD, HEAD), F32),
            pltpu.SemaphoreType.DMA((SEMS,)),
            pltpu.SemaphoreType.DMA((SEMS,)),
        ],
        compiler_params=pltpu.CompilerParams(
            collective_id=0, has_side_effects=True, vmem_limit_bytes=48 * 1024 * 1024
        ),
        name="attention_backward",
    )(
        table,
        live,
        columns,
        activations,
        queries,
        key_tensor,
        value_tensor,
        output_gradient,
    )
    return dq, dkv[0], dkv[1], dw[0], dw[1]


def solution(mesh):
    placed = (P("ctx", "tp"),) * 5 + (P(), P())
    return jax.shard_map(
        body,
        mesh=mesh,
        in_specs=placed,
        out_specs=(P("ctx", "tp"),) * 5,
        check_vma=False,
    )
```

```python
import functools
import math

import jax
import jax.numpy as jnp
from jax import lax
from jax.experimental import pallas as pl
from jax.experimental.pallas import tpu as pltpu
from jax.sharding import PartitionSpec as P

MESH = pl.DeviceIdType.MESH
F32 = jnp.float32
BF16 = jnp.bfloat16

HEAD = 128
BLOCK = 512
HALF = 256
PICKS = 3
CHIPS = 32
ROWS_Y = 4
ROWS_Z = 8
ROWS_X = 4
CLASSES = 16
REPLICAS = 2
PIECE = BLOCK // CLASSES
CHUNKS = 4
CHUNK = BLOCK // CHUNKS
HEADS = 4
QUERIES = HEADS * HALF
SCALE = HEAD**-0.5
EXP_SCALE = SCALE * math.log2(math.e)
LOW = -1e30

(LOAD, P1, OWN, ACT1, ACT3, HALVES, SUMS, LISTS, ORDER, DQ) = range(10)
P2 = 10
SWAP = P2 + PICKS
BACK0 = SWAP + PICKS
ALONG_X = BACK0 + PICKS + 1
BACK2 = ALONG_X + ROWS_X
BACK1 = BACK2 + PICKS
GATHER = BACK1 + CHUNKS
SEMS = GATHER + CHUNKS


def rows_dot(left, right):
    return lax.dot_general(left, right, (((1,), (1,)), ((), ())), preferred_element_type=F32)


def plain_dot(left, right):
    return lax.dot_general(left, right, (((1,), (0,)), ((), ())), preferred_element_type=F32)


def kernel(
    act_in,
    q_in,
    k_in,
    v_in,
    go_in,
    selection_in,
    order_in,
    dq_out,
    dkv_out,
    dw_out,
    qd,
    own,
    held,
    picked,
    kv,
    key_t,
    exps,
    gprobs,
    stats,
    factors,
    delta,
    low,
    cross,
    crossed,
    terms,
    landed,
    member,
    totals,
    sums,
    final,
    own_terms,
    dq_t,
    dq_rows,
    grads,
    all_grads,
    grads_t,
    acts,
    wide,
    w_send,
    wide_in,
    selection,
    order,
    inverse,
    table,
    send,
    recv,
):
    c = lax.axis_index("ctx")
    x = lax.axis_index("tp")
    chip = c // 2
    core = c % 2
    z = chip // ROWS_Y
    y = chip % ROWS_Y
    other = 1 - core
    sibling = c + 1 - 2 * core
    piece_class = chip % CLASSES
    first_z = z + ROWS_Z - 1 - core

    def remote(src, dst, sem, ctx, tp=None):
        return pltpu.make_async_remote_copy(
            src_ref=src,
            dst_ref=dst,
            send_sem=send.at[sem],
            recv_sem=recv.at[sem],
            device_id=(ctx, x if tp is None else tp),
            device_id_type=MESH,
        )

    def local(src, dst, sem):
        return pltpu.make_async_copy(src, dst, recv.at[sem])

    def put(src, dst, sem, ctx):
        @pl.when(ctx != c)
        def _():
            remote(src, dst, sem, ctx).start()

        @pl.when(ctx == c)
        def _():
            local(src, dst, sem).start()

    coming = {}
    leaving = []

    def expect(sem, arrives, leaves=None):
        coming[sem] = arrives
        if leaves is not None:
            leaving.append((sem, leaves))

    def take(ref, sem):
        pltpu.make_async_copy(ref, ref, recv.at[sem]).wait()

    def arrived(sem):
        take(coming.pop(sem), sem)

    def sent(ref, sem):
        pltpu.make_async_copy(ref, ref, send.at[sem]).wait()

    def finish():
        for sem in list(coming):
            arrived(sem)
        for sem, ref in leaving:
            if ref is held:
                here = piece_class // (CLASSES // 2) == core

                @pl.when(here)
                def _():
                    sent(ref.at[pl.ds(0, CHIPS - 1)], sem)

                @pl.when(jnp.logical_not(here))
                def _():
                    sent(ref, sem)
            else:
                sent(ref, sem)

    barrier = pltpu.get_barrier_semaphore()

    def greet(d, carry):
        pl.semaphore_signal(
            barrier, inc=1, device_id=(lax.rem(c + d, 2 * CHIPS), x), device_id_type=MESH
        )
        return carry

    lax.fori_loop(1, 2 * CHIPS, greet, 0)
    for d in range(1, ROWS_X):
        pl.semaphore_signal(
            barrier, inc=1, device_id=(c, lax.rem(x + d, ROWS_X)), device_id_type=MESH
        )

    local(selection_in, selection, LISTS).start()
    local(order_in, order, ORDER).start()
    expect(LISTS, selection)
    expect(ORDER, order)
    for h in range(HEADS):
        strip = pl.ds(h * HEAD, HEAD)
        block = pl.ds(h * HALF, HALF)
        local(q_in.at[:, strip], qd.at[0, block], LOAD).start()
        local(go_in.at[:, strip], qd.at[1, block], LOAD).start()
    expect(LOAD, qd)

    pl.semaphore_wait(barrier, 2 * CHIPS - 1 + ROWS_X - 1)

    def spread(j, carry):
        rows = pl.ds(pl.multiple_of(j * PIECE, PIECE), PIECE)
        for replica in range(REPLICAS):
            holder = core * (CLASSES // 2) + j + CLASSES * replica
            for kind, src in ((0, k_in), (1, v_in)):
                put(src.at[rows], held.at[chip], P1, holder * 2 + kind)
        return carry

    lax.fori_loop(0, CLASSES // 2, spread, 0)
    expect(P1, held, held)

    my_rows = pl.ds(pl.multiple_of(core * HALF, HALF), HALF)
    for kind, src in ((0, k_in), (1, v_in)):
        remote(src, own.at[kind, my_rows], OWN, sibling).start()
        local(src, own.at[kind, my_rows], OWN).start()
    expect(OWN, own, own.at[:, pl.ds(0, HALF)])

    for d in range(ROWS_Y):
        y_to = lax.rem(y + d, ROWS_Y)
        for s in range(2):
            src = act_in.at[:, pl.ds(pl.multiple_of((y_to + ROWS_Y * s) * HEAD, HEAD), HEAD)]
            dst = acts.at[x, core, y, :, pl.ds(s * HEAD, HEAD)]
            if d == 0:
                local(src, dst, ACT1).start()
            else:
                remote(src, dst, ACT1, (z * ROWS_Y + y_to) * 2 + core).start()
    expect(ACT1, acts.at[x, core], acts.at[0, 0, pl.ds(0, ROWS_Y - 1)])

    arrived(ORDER)
    arrived(LISTS)

    def invert(e, carry):
        at = jnp.int32(0)
        for b in range(CHIPS):
            at = jnp.where(order[b] == e, b, at)
        inverse[e] = at
        return carry

    lax.fori_loop(0, CHIPS, invert, 0)

    def look_up(t, carry):
        for j in range(PICKS):
            table[t, j] = inverse[selection[j, order[t]]]
        return carry

    lax.fori_loop(0, CHIPS, look_up, 0)
    arrived(P1)

    for j in range(PICKS):

        def serve(n, carry, j=j):
            z_to = lax.rem(first_z + n // ROWS_Y, ROWS_Z)
            target = z_to * ROWS_Y + lax.rem(y + n, ROWS_Y)
            picked[j, n] = held[table[target, j]]
            put(picked.at[j, n], kv.at[core, j, piece_class], P2 + j, target * 2 + core)
            return carry

        lax.fori_loop(0, CLASSES, serve, 0)
        expect(P2 + j, kv.at[core, j], kv.at[0, 0, pl.ds(0, CLASSES - 1)])

    arrived(ACT1)
    for d in range(1, ROWS_X):
        x_to = lax.rem(x + d, ROWS_X)
        remote(acts.at[x, core], acts.at[x, core], ALONG_X + d, c, x_to).start()
        x_from = lax.rem(x + ROWS_X - d, ROWS_X)
        expect(ALONG_X + d, acts.at[x_from, core], acts.at[0, 0])

    def lines(kind, j):
        if j == PICKS:
            return own[kind]
        return kv[kind, j].reshape(BLOCK, HEAD)

    def forward(j):
        keys = lines(0, j)
        values = lines(1, j)
        key_t[j] = keys.T

        def one_head(h, carry):
            block = pl.ds(pl.multiple_of(h * HALF, HALF), HALF)
            raw = rows_dot(keys, qd[0, block, :])
            if j == PICKS:
                key_at = lax.broadcasted_iota(jnp.int32, raw.shape, 0)
                query_at = lax.broadcasted_iota(jnp.int32, raw.shape, 1) + core * HALF
                raw = jnp.where(key_at <= query_at, raw, LOW)
            top = jnp.max(raw, axis=0, keepdims=True)
            weights = jnp.exp2((raw - top) * EXP_SCALE)
            gp = rows_dot(values, qd[1, block, :])
            exps[j, :, block] = weights
            gprobs[j, :, block] = gp
            stats[j, 0, :, block] = top
            stats[j, 1, :, block] = jnp.sum(weights, axis=0, keepdims=True)
            stats[j, 2, :, block] = jnp.sum(weights * gp, axis=0, keepdims=True)
            return carry

        lax.fori_loop(0, HEADS, one_head, 0)

    arrived(OWN)
    arrived(LOAD)
    forward(PICKS)

    column = lax.broadcasted_iota(jnp.int32, (1, BLOCK), 1)
    step_rows = 2 * PIECE
    row = lax.broadcasted_iota(jnp.int32, (step_rows, BLOCK), 0)
    same = jnp.where(
        row % PIECE == lax.broadcasted_iota(jnp.int32, (step_rows, BLOCK), 1) % PIECE, 1.0, 0.0
    )
    for j in range(PICKS):
        wanted = jnp.zeros((1, BLOCK), jnp.int32)
        for n in range(CLASSES):
            client = lax.rem(first_z + n // ROWS_Y, ROWS_Z) * ROWS_Y + n % ROWS_Y
            wanted = jnp.where(column // PIECE == n, table[client, j], wanted)

        def fill(r, carry, j=j, wanted=wanted):
            hit = row // PIECE + 2 * r == wanted
            at = pl.ds(pl.multiple_of(r * step_rows, step_rows), step_rows)
            member[j, at, :] = jnp.where(hit, same, 0.0).astype(BF16)
            return carry

        lax.fori_loop(0, CHIPS // 2, fill, 0)

    def swap(j):
        arrived(P2 + j)
        remote(kv.at[core, j], kv.at[core, j], SWAP + j, sibling).start()
        expect(SWAP + j, kv.at[other, j], kv.at[0, 0])

    swap(0)
    swap(1)
    arrived(SWAP)
    forward(0)
    swap(2)
    arrived(SWAP + 1)
    forward(1)
    arrived(SWAP + 2)
    forward(2)

    mine_at = order[chip]
    alive = [selection[j, mine_at] != mine_at for j in range(PICKS)] + [True]
    peak = stats[PICKS, 0]
    for j in range(PICKS):
        peak = jnp.maximum(peak, jnp.where(alive[j], stats[j, 0], LOW))
    total = jnp.zeros((1, QUERIES), F32)
    turned = jnp.zeros((1, QUERIES), F32)
    scaled = []
    for j in range(PICKS + 1):
        part = jnp.exp2(jnp.minimum(stats[j, 0] - peak, 0.0) * EXP_SCALE)
        part = jnp.where(alive[j], part, 0.0)
        scaled.append(part)
        total = total + part * stats[j, 1]
        turned = turned + part * stats[j, 2]
    share = 1.0 / total
    delta[...] = turned * share
    for j in range(PICKS + 1):
        factors[j] = scaled[j] * share

    mine_scale = jnp.where(core == 0, SCALE, 1.0).astype(F32)
    other_scale = jnp.where(core == 0, 1.0, SCALE).astype(F32)

    def backward(j):
        keys_t = key_t[j]

        def one_head(h, carry):
            block = pl.ds(pl.multiple_of(h * HALF, HALF), HALF)
            probs = exps[j, :, block] * factors[j, :, block]
            gs = (probs * (gprobs[j, :, block] - delta[:, block])).astype(BF16)
            low[1, j, :, block] = probs.astype(BF16)
            low[0, j, :, block] = gs
            dq = plain_dot(keys_t, gs)
            dq_t[:, block] = dq if j == 0 else dq_t[:, block] + dq
            return carry

        lax.fori_loop(0, HEADS, one_head, 0)
        cross[j] = (plain_dot(low[other, j], qd[other]) * other_scale).astype(BF16)
        remote(cross.at[j], crossed.at[j], BACK0 + j, sibling).start()
        expect(BACK0 + j, crossed.at[j], cross.at[j])

    def combine(j):
        mine = plain_dot(low[core, j], qd[core]) * mine_scale
        arrived(BACK0 + j)
        return mine + crossed[j].astype(F32)

    def give(j):
        terms[j] = combine(j).astype(BF16).reshape(CLASSES, PIECE, HEAD)

        def one(n, carry):
            w = n // ROWS_Y
            z_to = lax.rem(z + ROWS_Z + 1 + core - w, ROWS_Z)
            holder = z_to * ROWS_Y + lax.rem(y + n, ROWS_Y)
            src = terms.at[j, lax.rem(holder, CLASSES)]
            put(src, landed.at[j, w * ROWS_Y + y], BACK2 + j, holder * 2 + core)
            return carry

        lax.fori_loop(0, CLASSES, one, 0)
        expect(BACK2 + j, landed.at[j], terms.at[0, pl.ds(0, CLASSES - 1)])

    backward(0)
    backward(1)
    give(0)
    backward(2)
    give(1)
    backward(PICKS)
    give(2)
    own_terms[...] = combine(PICKS)

    for h in range(HEADS):
        dq = dq_t[:, pl.ds(h * HALF, HALF)] * SCALE
        dq_rows[:, pl.ds(h * HEAD, HEAD)] = dq.T.astype(BF16)
    local(dq_rows, dq_out, DQ).start()
    expect(DQ, dq_out)

    for d in range(1, ROWS_X):
        arrived(ALONG_X + d)
    remote(acts.at[:, core], acts.at[:, core], ACT3, sibling).start()
    expect(ACT3, acts.at[:, other], acts.at[:, 0])

    for j in range(PICKS):
        arrived(BACK2 + j)
        part = plain_dot(member[j], landed[j].reshape(BLOCK, HEAD))
        if j == 0:
            totals[...] = part
        elif j < PICKS - 1:
            totals[...] += part
        else:
            sums[...] = (totals[...] + part).astype(BF16).reshape(CHIPS, PIECE, HEAD)

    def give_back(d, carry):
        target = lax.rem(chip + d, CHIPS)
        put(sums.at[target], final.at[chip], BACK1 + z % CHUNKS, target * 2 + core)
        return carry

    lax.fori_loop(0, CHIPS, give_back, 0)
    leaving.append((BACK1 + z % CHUNKS, sums.at[pl.ds(0, CHIPS - 1)]))

    def chunk_of(step):
        g = lax.rem(z + (2, 1, 3, 0)[step], CHUNKS)
        return g, pl.ds(pl.multiple_of(g * CHUNK, CHUNK), CHUNK)

    def collect(step):
        g, rows = chunk_of(step)
        take(final.at[pl.ds(0, 2 * ROWS_Y)], BACK1 + g)
        near = final[pl.ds(g * ROWS_Y, ROWS_Y)].astype(F32)
        far = final[pl.ds(CLASSES + g * ROWS_Y, ROWS_Y)].astype(F32)
        both = (near + far).reshape(CHUNK, HEAD) + own_terms[rows, :]
        grads[rows, :] = both.astype(BF16)
        for d in range(ROWS_Y):
            y_to = lax.rem(y + d, ROWS_Y)
            dst = all_grads.at[y, rows]
            if d == 0:
                local(grads.at[rows], dst, GATHER + step).start()
            else:
                to = (z * ROWS_Y + y_to) * 2 + core
                remote(grads.at[rows], dst, GATHER + step, to).start()
        expect(
            GATHER + step,
            all_grads.at[:, rows],
            all_grads.at[pl.ds(0, ROWS_Y - 1), pl.ds(0, CHUNK)],
        )

    def project(step):
        g, rows = chunk_of(step)
        arrived(GATHER + step)
        for b in range(ROWS_Y):
            grads_t[:, pl.ds(b * CHUNK, CHUNK)] = all_grads[b, rows, :].T
        half_rows = pl.ds(pl.multiple_of((g % 2) * CHUNK, CHUNK), CHUNK)
        for o in (2, 1, 3, 0):
            a = lax.rem(z // 2 + o, ROWS_X)
            part = plain_dot(
                grads_t[...], acts[a, g // 2, :, half_rows, :].reshape(ROWS_Y * CHUNK, 2 * HEAD)
            )
            if step == 0:
                wide[a] = part
                continue
            if step < CHUNKS - 1:
                wide[a] += part
                continue
            part = part + wide[a]
            for s in range(2):
                z_to = 2 * a + s
                w_send[z_to] = part[:, s * HEAD : (s + 1) * HEAD].T.astype(BF16)
                for h in range(2):
                    src = w_send.at[z_to, pl.ds(h * (HEAD // 2), HEAD // 2)]
                    to = (z_to * ROWS_Y + y) * 2 + h
                    put(src, wide_in.at[core, z], SUMS, to)

    collect(0)
    collect(1)
    arrived(ACT3)
    project(0)
    collect(2)
    project(1)
    collect(3)
    their_rows = pl.ds(pl.multiple_of(other * HALF, HALF), HALF)
    remote(grads.at[their_rows], dkv_out.at[core], HALVES, sibling).start()
    local(grads.at[my_rows], dkv_out.at[core], HALVES).start()
    expect(HALVES, dkv_out, dkv_out.at[0])
    project(2)
    project(3)
    expect(SUMS, wide_in, totals.at[pl.ds(0, (2 * ROWS_Z - 1) * HEAD // 4)])
    arrived(SUMS)
    for kind in range(2):
        acc = wide_in[kind, 0].astype(F32)
        for d in range(1, ROWS_Z):
            acc = acc + wide_in[kind, d].astype(F32)
        dw_out[kind] = acc
    finish()


def copy_kernel(dq, dkv, dw, dq_out, dk_out, dv_out, dwk_out, dwv_out, sems):
    copies = [
        pltpu.make_async_copy(src, dst, sems.at[n])
        for n, (src, dst) in enumerate(
            (
                (dq, dq_out),
                (dkv.at[0], dk_out),
                (dkv.at[1], dv_out),
                (dw.at[0], dwk_out),
                (dw.at[1], dwv_out),
            )
        )
    ]
    for one in copies:
        one.start()
    for one in copies:
        one.wait()


def body(activations, queries, key_tensor, value_tensor, output_gradient, selection, block_order):
    vmem = pl.BlockSpec(memory_space=pltpu.VMEM)
    hbm = pl.BlockSpec(memory_space=pltpu.HBM)
    dq, dkv, dw = pl.pallas_call(
        kernel,
        out_shape=(
            jax.ShapeDtypeStruct((HALF, HEADS * HEAD), BF16),
            jax.ShapeDtypeStruct((2, HALF, HEAD), BF16),
            jax.ShapeDtypeStruct((2, HEAD // 2, HEAD), F32),
        ),
        in_specs=[hbm] * 7,
        out_specs=[hbm, hbm, vmem],
        scratch_shapes=[
            pltpu.VMEM((2, QUERIES, HEAD), BF16),
            pltpu.VMEM((2, BLOCK, HEAD), BF16),
            pltpu.VMEM((CHIPS, PIECE, HEAD), BF16),
            pltpu.VMEM((PICKS, CLASSES, PIECE, HEAD), BF16),
            pltpu.VMEM((2, PICKS, CLASSES, PIECE, HEAD), BF16),
            pltpu.VMEM((PICKS + 1, HEAD, BLOCK), BF16),
            pltpu.VMEM((PICKS + 1, BLOCK, QUERIES), F32),
            pltpu.VMEM((PICKS + 1, BLOCK, QUERIES), F32),
            pltpu.VMEM((PICKS + 1, 3, 1, QUERIES), F32),
            pltpu.VMEM((PICKS + 1, 1, QUERIES), F32),
            pltpu.VMEM((1, QUERIES), F32),
            pltpu.VMEM((2, PICKS + 1, BLOCK, QUERIES), BF16),
            pltpu.VMEM((PICKS + 1, BLOCK, HEAD), BF16),
            pltpu.VMEM((PICKS + 1, BLOCK, HEAD), BF16),
            pltpu.VMEM((PICKS, CLASSES, PIECE, HEAD), BF16),
            pltpu.VMEM((PICKS, CLASSES, PIECE, HEAD), BF16),
            pltpu.VMEM((PICKS, CHIPS * PIECE, BLOCK), BF16),
            pltpu.VMEM((CHIPS * PIECE, HEAD), F32),
            pltpu.VMEM((CHIPS, PIECE, HEAD), BF16),
            pltpu.VMEM((CHIPS, PIECE, HEAD), BF16),
            pltpu.VMEM((BLOCK, HEAD), F32),
            pltpu.VMEM((HEAD, QUERIES), F32),
            pltpu.VMEM((HALF, HEADS * HEAD), BF16),
            pltpu.VMEM((BLOCK, HEAD), BF16),
            pltpu.VMEM((ROWS_Y, BLOCK, HEAD), BF16),
            pltpu.VMEM((HEAD, ROWS_Y * CHUNK), BF16),
            pltpu.VMEM((ROWS_X, 2, ROWS_Y, HALF, 2 * HEAD), BF16),
            pltpu.VMEM((ROWS_X, HEAD, 2 * HEAD), F32),
            pltpu.VMEM((ROWS_Z, HEAD, HEAD), BF16),
            pltpu.VMEM((2, ROWS_Z, HEAD // 2, HEAD), BF16),
            pltpu.SMEM((PICKS, CHIPS), jnp.int32),
            pltpu.SMEM((CHIPS,), jnp.int32),
            pltpu.SMEM((CHIPS,), jnp.int32),
            pltpu.SMEM((CHIPS, PICKS), jnp.int32),
            pltpu.SemaphoreType.DMA((SEMS,)),
            pltpu.SemaphoreType.DMA((SEMS,)),
        ],
        compiler_params=pltpu.CompilerParams(
            collective_id=0, has_side_effects=True, vmem_limit_bytes=56 * 1024 * 1024
        ),
        name="attention_backward",
    )(
        activations,
        queries,
        key_tensor,
        value_tensor,
        output_gradient,
        selection.T,
        block_order,
    )
    shapes = (dq.shape, dkv.shape[1:], dkv.shape[1:], dw.shape[1:], dw.shape[1:])
    kinds = (BF16, BF16, BF16, F32, F32)
    return pl.pallas_call(
        copy_kernel,
        out_shape=tuple(jax.ShapeDtypeStruct(s, t) for s, t in zip(shapes, kinds)),
        in_specs=[hbm] * 3,
        out_specs=[hbm] * 5,
        scratch_shapes=[pltpu.SemaphoreType.DMA((5,))],
        name="copy_out",
    )(dq, dkv, dw)


def solution(mesh):
    placed = (P("ctx", "tp"),) * 5 + (P(), P())
    return jax.shard_map(
        body,
        mesh=mesh,
        in_specs=placed,
        out_specs=(P("ctx", "tp"),) * 5,
        check_vma=False,
    )
```

```python
import functools
import math

import jax
import jax.numpy as jnp
from jax import lax
from jax.experimental import pallas as pl
from jax.experimental.pallas import tpu as pltpu
from jax.sharding import PartitionSpec as P

MESH = pl.DeviceIdType.MESH
F32 = jnp.float32
BF16 = jnp.bfloat16

HEAD = 128
BLOCK = 512
HALF = 256
PICKS = 3
CHIPS = 32
ROWS_Y = 4
ROWS_Z = 8
ROWS_X = 4
CLASSES = 16
REPLICAS = 2
PIECE = HALF // CLASSES
CHUNKS = 4
CHUNK = HALF // CHUNKS
TERMS = CLASSES * PIECE
HEADS = 4
QUERIES = HEADS * BLOCK
SCALE = HEAD**-0.5
EXP_SCALE = SCALE * math.log2(math.e)
LOW = -1e30

(LOAD, P1, PACK, ACT1, ACT3, STATS, SUMS, LISTS, ORDER, DQ, DQ_PART, DKV) = range(12)
P2 = 12
ALONG_X = P2 + PICKS
BACK2 = ALONG_X + ROWS_X
BACK1 = BACK2 + PICKS
GATHER = BACK1 + CHUNKS
SEMS = GATHER + CHUNKS


def rows_dot(left, right):
    return lax.dot_general(left, right, (((1,), (1,)), ((), ())), preferred_element_type=F32)


def plain_dot(left, right):
    return lax.dot_general(left, right, (((1,), (0,)), ((), ())), preferred_element_type=F32)


def kernel(
    act_in,
    q_in,
    k_in,
    v_in,
    go_in,
    selection_in,
    order_in,
    dq_out,
    dkv_out,
    dw_out,
    qd,
    packed,
    held,
    picked,
    kv,
    key_t,
    exps,
    gprobs,
    stats,
    my_stats,
    their_stats,
    factors,
    delta,
    low,
    terms,
    landed,
    member,
    totals,
    sums,
    final,
    own_terms,
    dq_mine,
    dq_give,
    dq_got,
    dq_rows,
    grads,
    all_grads,
    grads_t,
    acts,
    wide,
    w_send,
    wide_in,
    selection,
    order,
    inverse,
    table,
    send,
    recv,
):
    c = lax.axis_index("ctx")
    x = lax.axis_index("tp")
    chip = c // 2
    core = c % 2
    z = chip // ROWS_Y
    y = chip % ROWS_Y
    other = 1 - core
    sibling = c + 1 - 2 * core
    piece_class = chip % CLASSES
    served = (2 + 4 * core, ROWS_Z - 1, 1, 0)

    def chip_at(dz, dy):
        return lax.rem(z + dz, ROWS_Z) * ROWS_Y + lax.rem(y + dy, ROWS_Y)

    def remote(src, dst, sem, ctx, tp=None):
        return pltpu.make_async_remote_copy(
            src_ref=src,
            dst_ref=dst,
            send_sem=send.at[sem],
            recv_sem=recv.at[sem],
            device_id=(ctx, x if tp is None else tp),
            device_id_type=MESH,
        )

    def local(src, dst, sem):
        return pltpu.make_async_copy(src, dst, recv.at[sem])

    def put(src, dst, sem, ctx, here):
        if here:
            local(src, dst, sem).start()
        else:
            remote(src, dst, sem, ctx).start()

    coming = {}
    leaving = []

    def expect(sem, arrives, leaves=None):
        coming[sem] = arrives
        if leaves is not None:
            leaving.append((sem, leaves))

    def take(ref, sem):
        pltpu.make_async_copy(ref, ref, recv.at[sem]).wait()

    def arrived(sem):
        take(coming.pop(sem), sem)

    def sent(ref, sem):
        pltpu.make_async_copy(ref, ref, send.at[sem]).wait()

    def finish():
        for sem in list(coming):
            arrived(sem)
        for sem, ref in leaving:
            sent(ref, sem)

    barrier = pltpu.get_barrier_semaphore()

    def greet(d, carry):
        pl.semaphore_signal(
            barrier, inc=1, device_id=(lax.rem(c + d, 2 * CHIPS), x), device_id_type=MESH
        )
        return carry

    lax.fori_loop(1, 2 * CHIPS, greet, 0)
    for d in range(1, ROWS_X):
        pl.semaphore_signal(
            barrier, inc=1, device_id=(c, lax.rem(x + d, ROWS_X)), device_id_type=MESH
        )

    local(selection_in, selection, LISTS).start()
    local(order_in, order, ORDER).start()
    expect(LISTS, selection)
    expect(ORDER, order)
    for kind, src in ((0, k_in), (1, v_in)):
        local(src, packed.at[:, kind], PACK).start()
    expect(PACK, packed)
    arrived(PACK)

    pl.semaphore_wait(barrier, 2 * CHIPS - 1 + ROWS_X - 1)

    far_first = (4, 3, 5, 2, 6, 1, 7, 0)
    for dz in far_first:
        for dy in (2, 1, 3, 0):
            target = chip_at(dz, dy)
            src = packed.at[lax.rem(target, CLASSES)]
            put(src, held.at[chip], P1, target * 2 + core, dz == 0 and dy == 0)
    expect(P1, held, held.at[pl.ds(0, CHIPS - 1)])

    for h in range(HEADS):
        strip = pl.ds(h * HEAD, HEAD)
        rows = pl.ds(pl.multiple_of(h * BLOCK + core * HALF, HALF), HALF)
        for kind, src in ((0, q_in), (1, go_in)):
            remote(src.at[:, strip], qd.at[kind, rows], LOAD, sibling).start()
            local(src.at[:, strip], qd.at[kind, rows], LOAD).start()
    expect(LOAD, qd, qd.at[0])

    arrived(ORDER)
    arrived(LISTS)

    def invert(e, carry):
        at = jnp.int32(0)
        for b in range(CHIPS):
            at = jnp.where(order[b] == e, b, at)
        inverse[e] = at
        return carry

    lax.fori_loop(0, CHIPS, invert, 0)

    def look_up(t, carry):
        for j in range(PICKS):
            table[t, j] = inverse[selection[j, order[t]]]
        return carry

    lax.fori_loop(0, CHIPS, look_up, 0)
    def lines(kind, j):
        source = packed if j == PICKS else kv.at[j]
        return source[:, kind].reshape(HALF, HEAD)

    def forward(j):
        keys = lines(0, j)
        values = lines(1, j)
        key_t[:, pl.ds(j * HALF, HALF)] = keys.T
        for h in range(HEADS):
            block = pl.ds(h * BLOCK, BLOCK)
            raw = rows_dot(keys, qd[0, block, :])
            if j == PICKS:
                key_at = lax.broadcasted_iota(jnp.int32, raw.shape, 0) + core * HALF
                query_at = lax.broadcasted_iota(jnp.int32, raw.shape, 1)
                raw = jnp.where(key_at <= query_at, raw, LOW)
            top = jnp.max(raw, axis=0, keepdims=True)
            weights = jnp.exp2((raw - top) * EXP_SCALE)
            gp = rows_dot(values, qd[1, block, :])
            exps[j, :, block] = weights
            gprobs[j, :, block] = gp
            stats[j, 0, :, block] = top
            stats[j, 1, :, block] = jnp.sum(weights, axis=0, keepdims=True)
            stats[j, 2, :, block] = jnp.sum(weights * gp, axis=0, keepdims=True)

    arrived(LOAD)
    forward(PICKS)

    for d in range(ROWS_Y):
        y_to = lax.rem(y + d, ROWS_Y)
        for s in range(2):
            src = act_in.at[:, pl.ds(pl.multiple_of((y_to + ROWS_Y * s) * HEAD, HEAD), HEAD)]
            dst = acts.at[x, core, y, :, pl.ds(s * HEAD, HEAD)]
            put(src, dst, ACT1, (z * ROWS_Y + y_to) * 2 + core, d == 0)
    expect(ACT1, acts.at[x, core], acts.at[0, 0, pl.ds(0, ROWS_Y - 1)])

    column = lax.broadcasted_iota(jnp.int32, (1, TERMS), 1)
    step_rows = 4 * PIECE
    row = lax.broadcasted_iota(jnp.int32, (step_rows, TERMS), 0)
    same = jnp.where(
        row % PIECE == lax.broadcasted_iota(jnp.int32, (step_rows, TERMS), 1) % PIECE, 1.0, 0.0
    )
    for j in range(PICKS):
        wanted = jnp.zeros((1, TERMS), jnp.int32)
        for n in range(CLASSES):
            client = chip_at(served[n // ROWS_Y], n % ROWS_Y)
            wanted = jnp.where(column // PIECE == n, table[client, j], wanted)

        def fill(r, carry, j=j, wanted=wanted):
            hit = row // PIECE + 4 * r == wanted
            at = pl.ds(pl.multiple_of(r * step_rows, step_rows), step_rows)
            member[j, at, :] = jnp.where(hit, same, 0.0).astype(BF16)
            return carry

        lax.fori_loop(0, CHIPS // 4, fill, 0)

    arrived(P1)

    for j in range(PICKS):
        for n in range(CLASSES):
            dz, dy = served[n // ROWS_Y], n % ROWS_Y
            target = chip_at(dz, dy)
            picked[j, n] = held[table[target, j]]
            dst = kv.at[j, piece_class]
            put(picked.at[j, n], dst, P2 + j, target * 2 + core, n == 3 * ROWS_Y)
        expect(P2 + j, kv.at[j], kv.at[0, pl.ds(0, CLASSES - 1)])

    arrived(ACT1)
    for d in range(1, ROWS_X):
        x_to = lax.rem(x + d, ROWS_X)
        remote(acts.at[x, core], acts.at[x, core], ALONG_X + d, c, x_to).start()
        x_from = lax.rem(x + ROWS_X - d, ROWS_X)
        expect(ALONG_X + d, acts.at[x_from, core], acts.at[0, 0])

    for j in range(PICKS):
        arrived(P2 + j)
        forward(j)

    mine_at = order[chip]
    alive = [selection[j, mine_at] != mine_at for j in range(PICKS)] + [True]

    def part_of(top, peak):
        return jnp.exp2(jnp.minimum(top - peak, 0.0) * EXP_SCALE)

    peak = stats[PICKS, 0]
    for j in range(PICKS):
        peak = jnp.maximum(peak, jnp.where(alive[j], stats[j, 0], LOW))
    total = jnp.zeros((1, QUERIES), F32)
    turned = jnp.zeros((1, QUERIES), F32)
    parts = []
    for j in range(PICKS + 1):
        part = jnp.where(alive[j], part_of(stats[j, 0], peak), 0.0)
        parts.append(part)
        total = total + part * stats[j, 1]
        turned = turned + part * stats[j, 2]
    my_stats[pl.ds(0, 1), :] = peak
    my_stats[pl.ds(1, 1), :] = total
    my_stats[pl.ds(2, 1), :] = turned
    remote(my_stats, their_stats, STATS, sibling).start()
    expect(STATS, their_stats, my_stats)
    arrived(STATS)
    their_peak = their_stats[pl.ds(0, 1), :]
    top = jnp.maximum(peak, their_peak)
    mine_part = part_of(peak, top)
    their_part = part_of(their_peak, top)
    share = 1.0 / (mine_part * total + their_part * their_stats[pl.ds(1, 1), :])
    delta[...] = (mine_part * turned + their_part * their_stats[pl.ds(2, 1), :]) * share
    for j in range(PICKS + 1):
        factors[j] = parts[j] * (mine_part * share)

    def backward(j):
        for h in range(HEADS):
            block = pl.ds(h * BLOCK, BLOCK)
            probs = exps[j, :, block] * factors[j, :, block]
            gs = probs * (gprobs[j, :, block] - delta[:, block])
            low[1, j, :, block] = probs.astype(BF16)
            low[0, j, :, block] = gs.astype(BF16)
        return plain_dot(low[0, j], qd[0]) * SCALE, plain_dot(low[1, j], qd[1])

    for j in range(PICKS):
        for kind, part in enumerate(backward(j)):
            terms[j, :, kind] = part.astype(BF16).reshape(CLASSES, PIECE, HEAD)
        for n in range(CLASSES):
            dz, dy = ROWS_Z - served[n // ROWS_Y], ROWS_Y - n % ROWS_Y
            holder = chip_at(dz, dy)
            src = terms.at[j, lax.rem(holder, CLASSES)]
            put(src, landed.at[j, n], BACK2 + j, holder * 2 + core, n == 3 * ROWS_Y)
        expect(BACK2 + j, landed.at[j], terms.at[0, pl.ds(0, CLASSES - 1)])
    for kind, part in enumerate(backward(PICKS)):
        own_terms[kind] = part

    for h in range(HEADS):
        gs = low[0, :, :, pl.ds(h * BLOCK, BLOCK)].reshape((PICKS + 1) * HALF, BLOCK)
        dq = plain_dot(key_t[...], gs)
        at = pl.ds(h * HALF, HALF)
        first, second = dq[:, :HALF], dq[:, HALF:]
        dq_mine[:, at] = jnp.where(core == 0, first, second)
        dq_give[:, at] = jnp.where(core == 0, second, first)
    remote(dq_give, dq_got, DQ_PART, sibling).start()
    expect(DQ_PART, dq_got, dq_give)

    for d in range(1, ROWS_X):
        arrived(ALONG_X + d)
    remote(acts.at[:, core], acts.at[:, core], ACT3, sibling).start()
    expect(ACT3, acts.at[:, other], acts.at[:, 0])

    for j in range(PICKS):
        arrived(BACK2 + j)
        both = [landed[j, :, kind].reshape(TERMS, HEAD) for kind in range(2)]
        part = plain_dot(member[j], jnp.concatenate(both, axis=1))
        if j == 0:
            totals[...] = part
        elif j < PICKS - 1:
            totals[...] += part
        else:
            part = (totals[...] + part).astype(BF16)
            for kind in range(2):
                strip = part[:, kind * HEAD : (kind + 1) * HEAD]
                sums[:, kind] = strip.reshape(CHIPS, PIECE, HEAD)

    group = z % CHUNKS
    for dz in (4, 0, 3, 7, 1, 5, 2, 6):
        for dy in (2, 1, 3, 0):
            target = chip_at(dz, dy)
            here = dz == 0 and dy == 0
            put(sums.at[target], final.at[chip], BACK1 + group, target * 2 + core, here)
    leaving.append((BACK1 + group, sums.at[pl.ds(0, CHIPS - 1)]))

    arrived(DQ_PART)
    for h in range(HEADS):
        at = pl.ds(h * HALF, HALF)
        dq = (dq_mine[:, at] + dq_got[:, at]) * SCALE
        dq_rows[:, pl.ds(h * HEAD, HEAD)] = dq.T.astype(BF16)
    local(dq_rows, dq_out, DQ).start()
    expect(DQ, dq_out)
    arrived(ACT3)

    def chunk_of(step):
        g = lax.rem(z + (0, 1, 3, 2)[step], CHUNKS)
        return g, pl.ds(pl.multiple_of(g * CHUNK, CHUNK), CHUNK)

    def collect(step):
        g, rows = chunk_of(step)
        take(final.at[pl.ds(0, 2 * ROWS_Y)], BACK1 + g)
        near = final[pl.ds(g * ROWS_Y, ROWS_Y)].astype(F32)
        far = final[pl.ds(CLASSES + g * ROWS_Y, ROWS_Y)].astype(F32)
        both = near + far
        for kind in range(2):
            whole = both[:, kind].reshape(CHUNK, HEAD) + own_terms[kind, rows, :]
            grads[kind, rows, :] = whole.astype(BF16)
        dst = all_grads.at[core, y, rows]
        for d in (2, 1, 3, 0):
            to = chip_at(0, d) * 2
            for swap in range(2):
                kind = core if swap == 0 else other
                put(grads.at[kind, rows], dst, GATHER + step, to + kind, d == 0 and swap == 0)
        expect(GATHER + step, all_grads.at[:, :, rows], held.at[pl.ds(0, 7 * CHUNK // (2 * PIECE))])

    def project(step):
        g, rows = chunk_of(step)
        arrived(GATHER + step)
        grads_t[...] = all_grads[:, :, rows, :].reshape(2 * ROWS_Y * CHUNK, HEAD).T
        for o in (2, 1, 3, 0):
            a = lax.rem(z // 2 + o, ROWS_X)
            features = acts[a, :, :, rows, :].reshape(2 * ROWS_Y * CHUNK, 2 * HEAD)
            part = plain_dot(grads_t[...], features)
            if step == 0:
                wide[a] = part
                continue
            if step < CHUNKS - 1:
                wide[a] += part
                continue
            part = part + wide[a]
            for s in range(2):
                z_to = 2 * a + s
                w_send[z_to] = part[:, s * HEAD : (s + 1) * HEAD].T.astype(BF16)
                for h in range(2):
                    src = w_send.at[z_to, pl.ds(h * (HEAD // 2), HEAD // 2)]
                    to = (z_to * ROWS_Y + y) * 2 + h
                    dst = wide_in.at[core, z]

                    @pl.when(to != c)
                    def _(src=src, dst=dst, to=to):
                        remote(src, dst, SUMS, to).start()

                    @pl.when(to == c)
                    def _(src=src, dst=dst):
                        local(src, dst, SUMS).start()

    for step in range(CHUNKS):
        collect(step)
    local(grads, dkv_out, DKV).start()
    expect(DKV, dkv_out)
    for step in range(CHUNKS - 1):
        project(step)
    project(3)
    expect(SUMS, wide_in, held.at[pl.ds(0, (2 * ROWS_Z - 1) * HEAD // (4 * PIECE))])
    arrived(SUMS)
    for kind in range(2):
        acc = wide_in[kind, 0].astype(F32)
        for d in range(1, ROWS_Z):
            acc = acc + wide_in[kind, d].astype(F32)
        dw_out[kind] = acc
    finish()


def copy_kernel(dq, dkv, dw, dq_out, dk_out, dv_out, dwk_out, dwv_out, sems):
    pairs = (
        (dq, dq_out),
        (dkv.at[0], dk_out),
        (dkv.at[1], dv_out),
        (dw.at[0], dwk_out),
        (dw.at[1], dwv_out),
    )
    copies = [pltpu.make_async_copy(src, dst, sems.at[n]) for n, (src, dst) in enumerate(pairs)]
    for one in copies:
        one.start()
    for one in copies:
        one.wait()


def body(activations, queries, key_tensor, value_tensor, output_gradient, selection, block_order):
    vmem = pl.BlockSpec(memory_space=pltpu.VMEM)
    hbm = pl.BlockSpec(memory_space=pltpu.HBM)
    dq, dkv, dw = pl.pallas_call(
        kernel,
        out_shape=(
            jax.ShapeDtypeStruct((HALF, HEADS * HEAD), BF16),
            jax.ShapeDtypeStruct((2, HALF, HEAD), BF16),
            jax.ShapeDtypeStruct((2, HEAD // 2, HEAD), F32),
        ),
        in_specs=[hbm] * 7,
        out_specs=[hbm, hbm, vmem],
        scratch_shapes=[
            pltpu.VMEM((2, QUERIES, HEAD), BF16),
            pltpu.VMEM((CLASSES, 2, PIECE, HEAD), BF16),
            pltpu.VMEM((CHIPS, 2, PIECE, HEAD), BF16),
            pltpu.VMEM((PICKS, CLASSES, 2, PIECE, HEAD), BF16),
            pltpu.VMEM((PICKS, CLASSES, 2, PIECE, HEAD), BF16),
            pltpu.VMEM((HEAD, (PICKS + 1) * HALF), BF16),
            pltpu.VMEM((PICKS + 1, HALF, QUERIES), F32),
            pltpu.VMEM((PICKS + 1, HALF, QUERIES), F32),
            pltpu.VMEM((PICKS + 1, 3, 1, QUERIES), F32),
            pltpu.VMEM((8, QUERIES), F32),
            pltpu.VMEM((8, QUERIES), F32),
            pltpu.VMEM((PICKS + 1, 1, QUERIES), F32),
            pltpu.VMEM((1, QUERIES), F32),
            pltpu.VMEM((2, PICKS + 1, HALF, QUERIES), BF16),
            pltpu.VMEM((PICKS, CLASSES, 2, PIECE, HEAD), BF16),
            pltpu.VMEM((PICKS, CLASSES, 2, PIECE, HEAD), BF16),
            pltpu.VMEM((PICKS, CHIPS * PIECE, TERMS), BF16),
            pltpu.VMEM((CHIPS * PIECE, 2 * HEAD), F32),
            pltpu.VMEM((CHIPS, 2, PIECE, HEAD), BF16),
            pltpu.VMEM((CHIPS, 2, PIECE, HEAD), BF16),
            pltpu.VMEM((2, HALF, HEAD), F32),
            pltpu.VMEM((HEAD, HEADS * HALF), F32),
            pltpu.VMEM((HEAD, HEADS * HALF), F32),
            pltpu.VMEM((HEAD, HEADS * HALF), F32),
            pltpu.VMEM((HALF, HEADS * HEAD), BF16),
            pltpu.VMEM((2, HALF, HEAD), BF16),
            pltpu.VMEM((2, ROWS_Y, HALF, HEAD), BF16),
            pltpu.VMEM((HEAD, 2 * ROWS_Y * CHUNK), BF16),
            pltpu.VMEM((ROWS_X, 2, ROWS_Y, HALF, 2 * HEAD), BF16),
            pltpu.VMEM((ROWS_X, HEAD, 2 * HEAD), F32),
            pltpu.VMEM((ROWS_Z, HEAD, HEAD), BF16),
            pltpu.VMEM((2, ROWS_Z, HEAD // 2, HEAD), BF16),
            pltpu.SMEM((PICKS, CHIPS), jnp.int32),
            pltpu.SMEM((CHIPS,), jnp.int32),
            pltpu.SMEM((CHIPS,), jnp.int32),
            pltpu.SMEM((CHIPS, PICKS), jnp.int32),
            pltpu.SemaphoreType.DMA((SEMS,)),
            pltpu.SemaphoreType.DMA((SEMS,)),
        ],
        compiler_params=pltpu.CompilerParams(
            collective_id=0, has_side_effects=True, vmem_limit_bytes=56 * 1024 * 1024
        ),
        name="attention_backward",
    )(
        activations,
        queries,
        key_tensor.reshape(CLASSES, PIECE, HEAD),
        value_tensor.reshape(CLASSES, PIECE, HEAD),
        output_gradient,
        selection.T,
        block_order,
    )
    shapes = (dq.shape, dkv.shape[1:], dkv.shape[1:], dw.shape[1:], dw.shape[1:])
    kinds = (BF16, BF16, BF16, F32, F32)
    return pl.pallas_call(
        copy_kernel,
        out_shape=tuple(jax.ShapeDtypeStruct(s, t) for s, t in zip(shapes, kinds)),
        in_specs=[hbm] * 3,
        out_specs=[vmem] * 5,
        scratch_shapes=[pltpu.SemaphoreType.DMA((5,))],
        name="copy_out",
    )(dq, dkv, dw)


def solution(mesh):
    placed = (P("ctx", "tp"),) * 5 + (P(), P())
    return jax.shard_map(
        body,
        mesh=mesh,
        in_specs=placed,
        out_specs=(P("ctx", "tp"),) * 5,
        check_vma=False,
    )
```

```python
import functools
import math

import jax
import jax.numpy as jnp
from jax import lax
from jax.experimental import pallas as pl
from jax.experimental.pallas import tpu as pltpu
from jax.sharding import PartitionSpec as P

MESH = pl.DeviceIdType.MESH
F32 = jnp.float32
BF16 = jnp.bfloat16

HEAD = 128
BLOCK = 512
HALF = 256
PICKS = 3
CHIPS = 32
ROWS_Y = 4
ROWS_Z = 8
ROWS_X = 4
CLASSES = 16
REPLICAS = 2
PIECE = HALF // CLASSES
CHUNKS = 4
CHUNK = HALF // CHUNKS
TERMS = CLASSES * PIECE
HEADS = 4
QUERIES = HEADS * BLOCK
SCALE = HEAD**-0.5
EXP_SCALE = SCALE * math.log2(math.e)
LOW = -1e30

(LOAD, P1, PACK, ACT1, ACT3, STATS, SUMS, LISTS, ORDER, DQ, DQ_PART, DKV) = range(12)
P2 = 12
ALONG_X = P2 + PICKS
BACK2 = ALONG_X + ROWS_X
BACK1 = BACK2 + PICKS
GATHER = BACK1 + CHUNKS
SEMS = GATHER + CHUNKS


def rows_dot(left, right):
    return lax.dot_general(left, right, (((1,), (1,)), ((), ())), preferred_element_type=F32)


def plain_dot(left, right):
    return lax.dot_general(left, right, (((1,), (0,)), ((), ())), preferred_element_type=F32)


def kernel(
    act_in,
    q_in,
    k_in,
    v_in,
    go_in,
    selection_in,
    order_in,
    dq_out,
    dkv_out,
    dw_out,
    qd,
    packed,
    held,
    picked,
    kv,
    key_t,
    exps,
    gprobs,
    stats,
    my_stats,
    their_stats,
    factors,
    delta,
    low,
    terms,
    landed,
    member,
    totals,
    sums,
    final,
    own_terms,
    dq_mine,
    dq_give,
    dq_got,
    dq_rows,
    grads,
    all_grads,
    grads_t,
    acts,
    wide,
    w_send,
    wide_in,
    selection,
    order,
    inverse,
    table,
    send,
    recv,
):
    c = lax.axis_index("ctx")
    x = lax.axis_index("tp")
    chip = c // 2
    core = c % 2
    z = chip // ROWS_Y
    y = chip % ROWS_Y
    other = 1 - core
    sibling = c + 1 - 2 * core
    piece_class = chip % CLASSES
    served = (2 + 4 * core, ROWS_Z - 1, 1, 0)

    def chip_at(dz, dy):
        return lax.rem(z + dz, ROWS_Z) * ROWS_Y + lax.rem(y + dy, ROWS_Y)

    def remote(src, dst, sem, ctx, tp=None):
        return pltpu.make_async_remote_copy(
            src_ref=src,
            dst_ref=dst,
            send_sem=send.at[sem],
            recv_sem=recv.at[sem],
            device_id=(ctx, x if tp is None else tp),
            device_id_type=MESH,
        )

    def local(src, dst, sem):
        return pltpu.make_async_copy(src, dst, recv.at[sem])

    def put(src, dst, sem, ctx, here):
        if here:
            local(src, dst, sem).start()
        else:
            remote(src, dst, sem, ctx).start()

    coming = {}
    leaving = []

    def expect(sem, arrives, leaves=None):
        coming[sem] = arrives
        if leaves is not None:
            leaving.append((sem, leaves))

    def take(ref, sem):
        pltpu.make_async_copy(ref, ref, recv.at[sem]).wait()

    def arrived(sem):
        take(coming.pop(sem), sem)

    def sent(ref, sem):
        pltpu.make_async_copy(ref, ref, send.at[sem]).wait()

    todo = []

    def finish():
        for st in todo:
            g, rows = chunk_of(st)
            take(final.at[pl.ds(0, 2 * ROWS_Y)], BACK1 + g)
        for sem in list(coming):
            arrived(sem)
        for sem, ref in leaving:
            sent(ref, sem)

    def chunk_of(step):
        g = lax.rem(z + (0, 1, 3, 2)[step], CHUNKS)
        return g, pl.ds(pl.multiple_of(g * CHUNK, CHUNK), CHUNK)

    barrier = pltpu.get_barrier_semaphore()

    def greet(d, carry):
        pl.semaphore_signal(
            barrier, inc=1, device_id=(lax.rem(c + d, 2 * CHIPS), x), device_id_type=MESH
        )
        return carry

    lax.fori_loop(1, 2 * CHIPS, greet, 0)
    for d in range(1, ROWS_X):
        pl.semaphore_signal(
            barrier, inc=1, device_id=(c, lax.rem(x + d, ROWS_X)), device_id_type=MESH
        )

    local(selection_in, selection, LISTS).start()
    local(order_in, order, ORDER).start()
    expect(LISTS, selection)
    expect(ORDER, order)
    for kind, src in ((0, k_in), (1, v_in)):
        local(src, packed.at[:, kind], PACK).start()
    expect(PACK, packed)
    arrived(PACK)

    pl.semaphore_wait(barrier, 2 * CHIPS - 1 + ROWS_X - 1)

    far_first = (4, 3, 5, 2, 6, 1, 7, 0)
    for dz in far_first:
        for dy in (2, 1, 3, 0):
            target = chip_at(dz, dy)
            src = packed.at[lax.rem(target, CLASSES)]
            put(src, held.at[chip], P1, target * 2 + core, dz == 0 and dy == 0)
    expect(P1, held, held.at[pl.ds(0, CHIPS - 1)])

    for d in range(ROWS_Y):
        y_to = lax.rem(y + d, ROWS_Y)
        for s in range(2):
            src = act_in.at[:, pl.ds(pl.multiple_of((y_to + ROWS_Y * s) * HEAD, HEAD), HEAD)]
            dst = acts.at[x, core, y, :, pl.ds(s * HEAD, HEAD)]
            put(src, dst, ACT1, (z * ROWS_Y + y_to) * 2 + core, d == 0)
    expect(ACT1, acts.at[x, core], acts.at[0, 0, pl.ds(0, ROWS_Y - 1)])

    for h in range(HEADS):
        strip = pl.ds(h * HEAD, HEAD)
        rows = pl.ds(pl.multiple_of(h * BLOCK + core * HALF, HALF), HALF)
        for kind, src in ((0, q_in), (1, go_in)):
            remote(src.at[:, strip], qd.at[kind, rows], LOAD, sibling).start()
            local(src.at[:, strip], qd.at[kind, rows], LOAD).start()
    expect(LOAD, qd, qd.at[0])

    arrived(ORDER)
    arrived(LISTS)

    def invert(e, carry):
        at = jnp.int32(0)
        for b in range(CHIPS):
            at = jnp.where(order[b] == e, b, at)
        inverse[e] = at
        return carry

    lax.fori_loop(0, CHIPS, invert, 0)

    def look_up(t, carry):
        for j in range(PICKS):
            table[t, j] = inverse[selection[j, order[t]]]
        return carry

    lax.fori_loop(0, CHIPS, look_up, 0)
    def lines(kind, j):
        source = packed if j == PICKS else kv.at[j]
        return source[:, kind].reshape(HALF, HEAD)

    def forward(j):
        keys = lines(0, j)
        values = lines(1, j)
        key_t[:, pl.ds(j * HALF, HALF)] = keys.T
        for h in range(HEADS):
            block = pl.ds(h * BLOCK, BLOCK)
            raw = rows_dot(keys, qd[0, block, :])
            if j == PICKS:
                key_at = lax.broadcasted_iota(jnp.int32, raw.shape, 0) + core * HALF
                query_at = lax.broadcasted_iota(jnp.int32, raw.shape, 1)
                raw = jnp.where(key_at <= query_at, raw, LOW)
            top = jnp.max(raw, axis=0, keepdims=True)
            weights = jnp.exp2((raw - top) * EXP_SCALE)
            gp = rows_dot(values, qd[1, block, :])
            exps[j, :, block] = weights
            gprobs[j, :, block] = gp
            stats[j, 0, :, block] = top
            stats[j, 1, :, block] = jnp.sum(weights, axis=0, keepdims=True)
            stats[j, 2, :, block] = jnp.sum(weights * gp, axis=0, keepdims=True)

    arrived(LOAD)
    forward(PICKS)

    column = lax.broadcasted_iota(jnp.int32, (1, TERMS), 1)
    step_rows = 4 * PIECE
    row = lax.broadcasted_iota(jnp.int32, (step_rows, TERMS), 0)
    same = jnp.where(
        row % PIECE == lax.broadcasted_iota(jnp.int32, (step_rows, TERMS), 1) % PIECE, 1.0, 0.0
    )
    for j in range(PICKS):
        wanted = jnp.zeros((1, TERMS), jnp.int32)
        for n in range(CLASSES):
            client = chip_at(served[n // ROWS_Y], n % ROWS_Y)
            wanted = jnp.where(column // PIECE == n, table[client, j], wanted)

        def fill(r, carry, j=j, wanted=wanted):
            hit = row // PIECE + 4 * r == wanted
            at = pl.ds(pl.multiple_of(r * step_rows, step_rows), step_rows)
            member[j, at, :] = jnp.where(hit, same, 0.0).astype(BF16)
            return carry

        lax.fori_loop(0, CHIPS // 4, fill, 0)

    arrived(P1)

    for j in range(PICKS):
        for n in range(CLASSES):
            dz, dy = served[n // ROWS_Y], n % ROWS_Y
            target = chip_at(dz, dy)
            picked[j, n] = held[table[target, j]]
            dst = kv.at[j, piece_class]
            put(picked.at[j, n], dst, P2 + j, target * 2 + core, n == 3 * ROWS_Y)
        expect(P2 + j, kv.at[j], kv.at[0, pl.ds(0, CLASSES - 1)])

    arrived(ACT1)
    for d in range(1, ROWS_X):
        x_to = lax.rem(x + d, ROWS_X)
        remote(acts.at[x, core], acts.at[x, core], ALONG_X + d, c, x_to).start()
        x_from = lax.rem(x + ROWS_X - d, ROWS_X)
        expect(ALONG_X + d, acts.at[x_from, core], acts.at[0, 0])

    arrived(P2)
    forward(0)
    arrived(P2 + 1)
    forward(1)
    arrived(P2+2)
    forward(2)

    mine_at = order[chip]
    alive = [selection[j, mine_at] != mine_at for j in range(PICKS)] + [True]

    def part_of(top, peak):
        return jnp.exp2(jnp.minimum(top - peak, 0.0) * EXP_SCALE)

    peak = stats[PICKS, 0]
    for j in range(PICKS):
        peak = jnp.maximum(peak, jnp.where(alive[j], stats[j, 0], LOW))
    total = jnp.zeros((1, QUERIES), F32)
    turned = jnp.zeros((1, QUERIES), F32)
    parts = []
    for j in range(PICKS + 1):
        part = jnp.where(alive[j], part_of(stats[j, 0], peak), 0.0)
        parts.append(part)
        total = total + part * stats[j, 1]
        turned = turned + part * stats[j, 2]
    my_stats[pl.ds(0, 1), :] = peak
    my_stats[pl.ds(1, 1), :] = total
    my_stats[pl.ds(2, 1), :] = turned
    remote(my_stats, their_stats, STATS, sibling).start()
    expect(STATS, their_stats, my_stats)
    arrived(STATS)
    their_peak = their_stats[pl.ds(0, 1), :]
    top = jnp.maximum(peak, their_peak)
    mine_part = part_of(peak, top)
    their_part = part_of(their_peak, top)
    share = 1.0 / (mine_part * total + their_part * their_stats[pl.ds(1, 1), :])
    delta[...] = (mine_part * turned + their_part * their_stats[pl.ds(2, 1), :]) * share
    for j in range(PICKS + 1):
        factors[j] = parts[j] * (mine_part * share)

    def backward(j):
        for h in range(HEADS):
            block = pl.ds(h * BLOCK, BLOCK)
            probs = exps[j, :, block] * factors[j, :, block]
            gs = probs * (gprobs[j, :, block] - delta[:, block])
            low[1, j, :, block] = probs.astype(BF16)
            low[0, j, :, block] = gs.astype(BF16)
        return plain_dot(low[0, j], qd[0]) * SCALE, plain_dot(low[1, j], qd[1])

    for j in range(PICKS):
        for kind, part in enumerate(backward(j)):
            terms[j, :, kind] = part.astype(BF16).reshape(CLASSES, PIECE, HEAD)
        for n in range(CLASSES):
            dz, dy = ROWS_Z - served[n // ROWS_Y], ROWS_Y - n % ROWS_Y
            holder = chip_at(dz, dy)
            src = terms.at[j, lax.rem(holder, CLASSES)]
            put(src, landed.at[j, n], BACK2 + j, holder * 2 + core, n == 3 * ROWS_Y)
        expect(BACK2 + j, landed.at[j], terms.at[0, pl.ds(0, CLASSES - 1)])
    for kind, part in enumerate(backward(PICKS)):
        own_terms[kind] = part

    for h in range(HEADS):
        gs = low[0, :, :, pl.ds(h * BLOCK, BLOCK)].reshape((PICKS + 1) * HALF, BLOCK)
        dq = plain_dot(key_t[...], gs)
        at = pl.ds(h * HALF, HALF)
        first, second = dq[:, :HALF], dq[:, HALF:]
        dq_mine[:, at] = jnp.where(core == 0, first, second)
        dq_give[:, at] = jnp.where(core == 0, second, first)
    remote(dq_give, dq_got, DQ_PART, sibling).start()
    expect(DQ_PART, dq_got, dq_give)

    for j in range(PICKS):
        arrived(BACK2 + j)
        both = [landed[j, :, kind].reshape(TERMS, HEAD) for kind in range(2)]
        part = plain_dot(member[j], jnp.concatenate(both, axis=1))
        if j == 0:
            totals[...] = part
        elif j < PICKS - 1:
            totals[...] += part
        else:
            part = (totals[...] + part).astype(BF16)
            for kind in range(2):
                strip = part[:, kind * HEAD : (kind + 1) * HEAD]
                sums[:, kind] = strip.reshape(CHIPS, PIECE, HEAD)

    group = z % CHUNKS
    for dz in (4, 0, 3, 7, 1, 5, 2, 6):
        for dy in (2, 1, 3, 0):
            target = chip_at(dz, dy)
            here = dz == 0 and dy == 0
            put(sums.at[target], final.at[chip], BACK1 + group, target * 2 + core, here)
    leaving.append((BACK1 + group, sums.at[pl.ds(0, CHIPS - 1)]))
    todo.extend(range(4))

    arrived(DQ_PART)
    for h in range(HEADS):
        at = pl.ds(h * HALF, HALF)
        dq = (dq_mine[:, at] + dq_got[:, at]) * SCALE
        dq_rows[:, pl.ds(h * HEAD, HEAD)] = dq.T.astype(BF16)
    local(dq_rows, dq_out, DQ).start()
    expect(DQ, dq_out)
    for d in range(1, ROWS_X):
        arrived(ALONG_X + d)
    remote(acts.at[:, core], acts.at[:, core], ACT3, sibling).start()
    expect(ACT3, acts.at[:, other], acts.at[:, 0])

    def collect(step):
        g, rows = chunk_of(step)
        take(final.at[pl.ds(0, 2 * ROWS_Y)], BACK1 + g)
        todo.remove(step)
        near = final[pl.ds(g * ROWS_Y, ROWS_Y)].astype(F32)
        far = final[pl.ds(CLASSES + g * ROWS_Y, ROWS_Y)].astype(F32)
        both = near + far
        for kind in range(2):
            whole = both[:, kind].reshape(CHUNK, HEAD) + own_terms[kind, rows, :]
            grads[kind, rows, :] = whole.astype(BF16)
        dst = all_grads.at[core, y, rows]
        for d in (2, 1, 3, 0):
            to = chip_at(0, d) * 2
            for swap in range(2):
                kind = core if swap == 0 else other
                put(grads.at[kind, rows], dst, GATHER + step, to + kind, d == 0 and swap == 0)
        expect(GATHER + step, all_grads.at[:, :, rows], held.at[pl.ds(0, 7 * CHUNK // (2 * PIECE))])

    def project(step):
        g, rows = chunk_of(step)
        arrived(GATHER + step)
        grads_t[...] = all_grads[:, :, rows, :].reshape(2 * ROWS_Y * CHUNK, HEAD).T
        for o in (2, 1, 3, 0):
            a = lax.rem(z // 2 + o, ROWS_X)
            features = acts[a, :, :, rows, :].reshape(2 * ROWS_Y * CHUNK, 2 * HEAD)
            part = plain_dot(grads_t[...], features)
            if step == 0:
                wide[a] = part
                continue
            if step < CHUNKS - 1:
                wide[a] += part
                continue
            part = part + wide[a]
            for s in range(2):
                z_to = 2 * a + s
                w_send[z_to] = part[:, s * HEAD : (s + 1) * HEAD].T.astype(BF16)
                for h in range(2):
                    src = w_send.at[z_to, pl.ds(h * (HEAD // 2), HEAD // 2)]
                    to = (z_to * ROWS_Y + y) * 2 + h
                    dst = wide_in.at[core, z]

                    @pl.when(to != c)
                    def _(src=src, dst=dst, to=to):
                        remote(src, dst, SUMS, to).start()

                    @pl.when(to == c)
                    def _(src=src, dst=dst):
                        local(src, dst, SUMS).start()

    collect(0)
    collect(1)
    collect(2)
    collect(3)
    local(grads, dkv_out, DKV).start()
    expect(DKV, dkv_out)
    arrived(ACT3)
    for step in range(CHUNKS - 1):
        project(step)
    project(3)
    expect(SUMS, wide_in, held.at[pl.ds(0, (2 * ROWS_Z - 1) * HEAD // (4 * PIECE))])
    arrived(SUMS)
    for kind in range(2):
        acc = wide_in[kind, 0].astype(F32)
        for d in range(1, ROWS_Z):
            acc = acc + wide_in[kind, d].astype(F32)
        dw_out[kind] = acc
    finish()


def copy_kernel(dq, dkv, dw, dq_out, dk_out, dv_out, dwk_out, dwv_out, sems):
    pairs = (
        (dq, dq_out),
        (dkv.at[0], dk_out),
        (dkv.at[1], dv_out),
        (dw.at[0], dwk_out),
        (dw.at[1], dwv_out),
    )
    copies = [pltpu.make_async_copy(src, dst, sems.at[n]) for n, (src, dst) in enumerate(pairs)]
    for one in copies:
        one.start()
    for one in copies:
        one.wait()


def body(activations, queries, key_tensor, value_tensor, output_gradient, selection, block_order):
    vmem = pl.BlockSpec(memory_space=pltpu.VMEM)
    hbm = pl.BlockSpec(memory_space=pltpu.HBM)
    dq, dkv, dw = pl.pallas_call(
        kernel,
        out_shape=(
            jax.ShapeDtypeStruct((HALF, HEADS * HEAD), BF16),
            jax.ShapeDtypeStruct((2, HALF, HEAD), BF16),
            jax.ShapeDtypeStruct((2, HEAD // 2, HEAD), F32),
        ),
        in_specs=[hbm] * 7,
        out_specs=[hbm, hbm, vmem],
        scratch_shapes=[
            pltpu.VMEM((2, QUERIES, HEAD), BF16),
            pltpu.VMEM((CLASSES, 2, PIECE, HEAD), BF16),
            pltpu.VMEM((CHIPS, 2, PIECE, HEAD), BF16),
            pltpu.VMEM((PICKS, CLASSES, 2, PIECE, HEAD), BF16),
            pltpu.VMEM((PICKS, CLASSES, 2, PIECE, HEAD), BF16),
            pltpu.VMEM((HEAD, (PICKS + 1) * HALF), BF16),
            pltpu.VMEM((PICKS + 1, HALF, QUERIES), F32),
            pltpu.VMEM((PICKS + 1, HALF, QUERIES), F32),
            pltpu.VMEM((PICKS + 1, 3, 1, QUERIES), F32),
            pltpu.VMEM((8, QUERIES), F32),
            pltpu.VMEM((8, QUERIES), F32),
            pltpu.VMEM((PICKS + 1, 1, QUERIES), F32),
            pltpu.VMEM((1, QUERIES), F32),
            pltpu.VMEM((2, PICKS + 1, HALF, QUERIES), BF16),
            pltpu.VMEM((PICKS, CLASSES, 2, PIECE, HEAD), BF16),
            pltpu.VMEM((PICKS, CLASSES, 2, PIECE, HEAD), BF16),
            pltpu.VMEM((PICKS, CHIPS * PIECE, TERMS), BF16),
            pltpu.VMEM((CHIPS * PIECE, 2 * HEAD), F32),
            pltpu.VMEM((CHIPS, 2, PIECE, HEAD), BF16),
            pltpu.VMEM((CHIPS, 2, PIECE, HEAD), BF16),
            pltpu.VMEM((2, HALF, HEAD), F32),
            pltpu.VMEM((HEAD, HEADS * HALF), F32),
            pltpu.VMEM((HEAD, HEADS * HALF), F32),
            pltpu.VMEM((HEAD, HEADS * HALF), F32),
            pltpu.VMEM((HALF, HEADS * HEAD), BF16),
            pltpu.VMEM((2, HALF, HEAD), BF16),
            pltpu.VMEM((2, ROWS_Y, HALF, HEAD), BF16),
            pltpu.VMEM((HEAD, 2 * ROWS_Y * CHUNK), BF16),
            pltpu.VMEM((ROWS_X, 2, ROWS_Y, HALF, 2 * HEAD), BF16),
            pltpu.VMEM((ROWS_X, HEAD, 2 * HEAD), F32),
            pltpu.VMEM((ROWS_Z, HEAD, HEAD), BF16),
            pltpu.VMEM((2, ROWS_Z, HEAD // 2, HEAD), BF16),
            pltpu.SMEM((PICKS, CHIPS), jnp.int32),
            pltpu.SMEM((CHIPS,), jnp.int32),
            pltpu.SMEM((CHIPS,), jnp.int32),
            pltpu.SMEM((CHIPS, PICKS), jnp.int32),
            pltpu.SemaphoreType.DMA((SEMS,)),
            pltpu.SemaphoreType.DMA((SEMS,)),
        ],
        compiler_params=pltpu.CompilerParams(
            collective_id=0, has_side_effects=True, vmem_limit_bytes=56 * 1024 * 1024
        ),
        name="attention_backward",
    )(
        activations,
        queries,
        key_tensor.reshape(CLASSES, PIECE, HEAD),
        value_tensor.reshape(CLASSES, PIECE, HEAD),
        output_gradient,
        selection.T,
        block_order,
    )
    shapes = (dq.shape, dkv.shape[1:], dkv.shape[1:], dw.shape[1:], dw.shape[1:])
    kinds = (BF16, BF16, BF16, F32, F32)
    return pl.pallas_call(
        copy_kernel,
        out_shape=tuple(jax.ShapeDtypeStruct(s, t) for s, t in zip(shapes, kinds)),
        in_specs=[hbm] * 3,
        out_specs=[vmem] * 5,
        scratch_shapes=[pltpu.SemaphoreType.DMA((5,))],
        name="copy_out",
    )(dq, dkv, dw)


def solution(mesh):
    placed = (P("ctx", "tp"),) * 5 + (P(), P())
    return jax.shard_map(
        body,
        mesh=mesh,
        in_specs=placed,
        out_specs=(P("ctx", "tp"),) * 5,
        check_vma=False,
    )
```

```python
import functools
import math

import jax
import jax.numpy as jnp
from jax import lax
from jax.experimental import pallas as pl
from jax.experimental.pallas import tpu as pltpu
from jax.sharding import PartitionSpec as P

MESH = pl.DeviceIdType.MESH
F32 = jnp.float32
BF16 = jnp.bfloat16

HEAD = 128
BLOCK = 512
HALF = 256
PICKS = 3
CHIPS = 32
ROWS_Y = 4
ROWS_Z = 8
ROWS_X = 4
CLASSES = 16
REPLICAS = 2
PIECE = HALF // CLASSES
CHUNKS = 4
CHUNK = HALF // CHUNKS
TERMS = CLASSES * PIECE
HEADS = 4
QUERIES = HEADS * BLOCK
SCALE = HEAD**-0.5
EXP_SCALE = SCALE * math.log2(math.e)
LOW = -1e30

(LOAD, P1, PACK, ACT1, STATS, SUMS, LISTS, ORDER, DQ, DQ_PART, DKV) = range(11)
P2 = 11
ALONG_X = P2 + PICKS
BACK2 = ALONG_X + ROWS_X
BACK1 = BACK2 + PICKS
GATHER = BACK1 + CHUNKS
ACROSS = GATHER + CHUNKS
SEMS = ACROSS + ROWS_X


def rows_dot(left, right):
    return lax.dot_general(left, right, (((1,), (1,)), ((), ())), preferred_element_type=F32)


def plain_dot(left, right):
    return lax.dot_general(left, right, (((1,), (0,)), ((), ())), preferred_element_type=F32)


def kernel(
    act_in,
    q_in,
    k_in,
    v_in,
    go_in,
    selection_in,
    order_in,
    dq_out,
    dkv_out,
    dw_out,
    qd,
    packed,
    held,
    picked,
    kv,
    key_t,
    exps,
    gprobs,
    stats,
    my_stats,
    their_stats,
    factors,
    delta,
    low,
    terms,
    landed,
    member,
    totals,
    sums,
    final,
    own_terms,
    dq_mine,
    dq_give,
    dq_got,
    dq_rows,
    grads,
    all_grads,
    grads_t,
    acts,
    wide,
    w_send,
    wide_in,
    selection,
    order,
    inverse,
    table,
    send,
    recv,
):
    c = lax.axis_index("ctx")
    x = lax.axis_index("tp")
    chip = c // 2
    core = c % 2
    z = chip // ROWS_Y
    y = chip % ROWS_Y
    other = 1 - core
    sibling = c + 1 - 2 * core
    piece_class = chip % CLASSES
    served = (2 + 4 * core, ROWS_Z - 1, 1, 0)

    def chip_at(dz, dy):
        return lax.rem(z + dz, ROWS_Z) * ROWS_Y + lax.rem(y + dy, ROWS_Y)

    def remote(src, dst, sem, ctx, tp=None):
        return pltpu.make_async_remote_copy(
            src_ref=src,
            dst_ref=dst,
            send_sem=send.at[sem],
            recv_sem=recv.at[sem],
            device_id=(ctx, x if tp is None else tp),
            device_id_type=MESH,
        )

    def local(src, dst, sem):
        return pltpu.make_async_copy(src, dst, recv.at[sem])

    def put(src, dst, sem, ctx, here):
        if here:
            local(src, dst, sem).start()
        else:
            remote(src, dst, sem, ctx).start()

    coming = {}
    leaving = []

    def expect(sem, arrives, leaves=None):
        coming[sem] = arrives
        if leaves is not None:
            leaving.append((sem, leaves))

    def take(ref, sem):
        pltpu.make_async_copy(ref, ref, recv.at[sem]).wait()

    def arrived(sem):
        take(coming.pop(sem), sem)

    def sent(ref, sem):
        pltpu.make_async_copy(ref, ref, send.at[sem]).wait()

    todo = []

    def finish():
        for st in todo:
            g, rows = chunk_of(st)
            take(final.at[pl.ds(0, 2 * ROWS_Y)], BACK1 + g)
        for sem in list(coming):
            arrived(sem)
        for sem, ref in leaving:
            sent(ref, sem)

    def chunk_of(step):
        g = lax.rem(z + (0, 1, 3, 2)[step], CHUNKS)
        return g, pl.ds(pl.multiple_of(g * CHUNK, CHUNK), CHUNK)

    barrier = pltpu.get_barrier_semaphore()

    def hello(ctx, tp=None):
        pl.semaphore_signal(
            barrier, inc=1, device_id=(ctx, x if tp is None else tp), device_id_type=MESH
        )

    far_first = (4, 3, 5, 2, 6, 1, 7, 0)
    peers = 0
    for dz in far_first:
        for dy in (2, 1, 3, 0):
            if dz or dy:
                hello(chip_at(dz, dy) * 2 + core)
                peers += 1
            if dz == 0 or dy == 0:
                hello(chip_at(dz, dy) * 2 + other)
                peers += 1
    for d in range(1, ROWS_X):
        hello(c, lax.rem(x + d, ROWS_X))
        peers += 1

    local(selection_in, selection, LISTS).start()
    local(order_in, order, ORDER).start()
    expect(LISTS, selection)
    expect(ORDER, order)
    for kind, src in ((0, k_in), (1, v_in)):
        local(src, packed.at[:, kind], PACK).start()
    expect(PACK, packed)
    arrived(PACK)

    pl.semaphore_wait(barrier, peers)

    for dz in far_first:
        for dy in (2, 1, 3, 0):
            target = chip_at(dz, dy)
            src = packed.at[lax.rem(target, CLASSES)]
            put(src, held.at[chip], P1, target * 2 + core, dz == 0 and dy == 0)
    expect(P1, held, held.at[pl.ds(0, CHIPS - 1)])

    for d in range(ROWS_Y):
        y_to = lax.rem(y + d, ROWS_Y)
        for s in range(2):
            src = act_in.at[:, pl.ds(pl.multiple_of((y_to + ROWS_Y * s) * HEAD, HEAD), HEAD)]
            dst = acts.at[x, core, y, :, pl.ds(s * HEAD, HEAD)]
            put(src, dst, ACT1, (z * ROWS_Y + y_to) * 2 + core, d == 0)
    expect(ACT1, acts.at[x, core], acts.at[0, 0, pl.ds(0, ROWS_Y - 1)])

    for h in range(HEADS):
        strip = pl.ds(h * HEAD, HEAD)
        rows = pl.ds(pl.multiple_of(h * BLOCK + core * HALF, HALF), HALF)
        for kind, src in ((0, q_in), (1, go_in)):
            remote(src.at[:, strip], qd.at[kind, rows], LOAD, sibling).start()
            local(src.at[:, strip], qd.at[kind, rows], LOAD).start()
    expect(LOAD, qd, qd.at[0])

    arrived(ORDER)
    arrived(LISTS)

    def invert(e, carry):
        at = jnp.int32(0)
        for b in range(CHIPS):
            at = jnp.where(order[b] == e, b, at)
        inverse[e] = at
        return carry

    lax.fori_loop(0, CHIPS, invert, 0)

    def look_up(t, carry):
        for j in range(PICKS):
            table[t, j] = inverse[selection[j, order[t]]]
        return carry

    lax.fori_loop(0, CHIPS, look_up, 0)
    def lines(kind, j):
        source = packed if j == PICKS else kv.at[j]
        return source[:, kind].reshape(HALF, HEAD)

    def forward(j):
        keys = lines(0, j)
        values = lines(1, j)
        key_t[:, pl.ds(j * HALF, HALF)] = keys.T
        for h in range(HEADS):
            block = pl.ds(h * BLOCK, BLOCK)
            raw = rows_dot(keys, qd[0, block, :])
            if j == PICKS:
                key_at = lax.broadcasted_iota(jnp.int32, raw.shape, 0) + core * HALF
                query_at = lax.broadcasted_iota(jnp.int32, raw.shape, 1)
                raw = jnp.where(key_at <= query_at, raw, LOW)
            top = jnp.max(raw, axis=0, keepdims=True)
            weights = jnp.exp2((raw - top) * EXP_SCALE)
            gp = rows_dot(values, qd[1, block, :])
            exps[j, :, block] = weights
            gprobs[j, :, block] = gp
            stats[j, 0, :, block] = top
            stats[j, 1, :, block] = jnp.sum(weights, axis=0, keepdims=True)
            stats[j, 2, :, block] = jnp.sum(weights * gp, axis=0, keepdims=True)


    arrived(P1)

    for j in range(PICKS):
        for n in range(CLASSES):
            dz, dy = served[n // ROWS_Y], n % ROWS_Y
            target = chip_at(dz, dy)
            picked[j, n] = held[table[target, j]]
            dst = kv.at[j, piece_class]
            put(picked.at[j, n], dst, P2 + j, target * 2 + core, n == 3 * ROWS_Y)
        expect(P2 + j, kv.at[j], kv.at[0, pl.ds(0, CLASSES - 1)])

    def across(d):
        x_from = lax.rem(x + ROWS_X - d, ROWS_X)
        remote(acts.at[x_from, core], acts.at[x_from, core], ACROSS + d, sibling).start()
        expect(ACROSS + d, acts.at[x_from, other], acts.at[0, 0])

    arrived(ACT1)
    for d in (1, 3):
        x_to = lax.rem(x + d, ROWS_X)
        remote(acts.at[x, core], acts.at[x, core], ALONG_X + d, c, x_to).start()
        x_from = lax.rem(x + ROWS_X - d, ROWS_X)
        expect(ALONG_X + d, acts.at[x_from, core], acts.at[0, 0])
    across(0)
    arrived(LOAD)
    forward(PICKS)

    column = lax.broadcasted_iota(jnp.int32, (1, TERMS), 1)
    step_rows = 4 * PIECE
    row = lax.broadcasted_iota(jnp.int32, (step_rows, TERMS), 0)
    same = jnp.where(
        row % PIECE == lax.broadcasted_iota(jnp.int32, (step_rows, TERMS), 1) % PIECE, 1.0, 0.0
    )
    for j in range(PICKS):
        wanted = jnp.zeros((1, TERMS), jnp.int32)
        for n in range(CLASSES):
            client = chip_at(served[n // ROWS_Y], n % ROWS_Y)
            wanted = jnp.where(column // PIECE == n, table[client, j], wanted)

        def fill(r, carry, j=j, wanted=wanted):
            hit = row // PIECE + 4 * r == wanted
            at = pl.ds(pl.multiple_of(r * step_rows, step_rows), step_rows)
            member[j, at, :] = jnp.where(hit, same, 0.0).astype(BF16)
            return carry

        lax.fori_loop(0, CHIPS // 4, fill, 0)


    arrived(P2)
    forward(0)
    arrived(P2 + 1)
    forward(1)
    arrived(P2+2)
    forward(2)

    mine_at = order[chip]
    alive = [selection[j, mine_at] != mine_at for j in range(PICKS)] + [True]

    def part_of(top, peak):
        return jnp.exp2(jnp.minimum(top - peak, 0.0) * EXP_SCALE)

    peak = stats[PICKS, 0]
    for j in range(PICKS):
        peak = jnp.maximum(peak, jnp.where(alive[j], stats[j, 0], LOW))
    total = jnp.zeros((1, QUERIES), F32)
    turned = jnp.zeros((1, QUERIES), F32)
    parts = []
    for j in range(PICKS + 1):
        part = jnp.where(alive[j], part_of(stats[j, 0], peak), 0.0)
        parts.append(part)
        total = total + part * stats[j, 1]
        turned = turned + part * stats[j, 2]
    my_stats[pl.ds(0, 1), :] = peak
    my_stats[pl.ds(1, 1), :] = total
    my_stats[pl.ds(2, 1), :] = turned
    remote(my_stats, their_stats, STATS, sibling).start()
    expect(STATS, their_stats, my_stats)
    arrived(STATS)
    their_peak = their_stats[pl.ds(0, 1), :]
    top = jnp.maximum(peak, their_peak)
    mine_part = part_of(peak, top)
    their_part = part_of(their_peak, top)
    share = 1.0 / (mine_part * total + their_part * their_stats[pl.ds(1, 1), :])
    delta[...] = (mine_part * turned + their_part * their_stats[pl.ds(2, 1), :]) * share
    for j in range(PICKS + 1):
        factors[j] = parts[j] * (mine_part * share)

    def backward(j):
        for h in range(HEADS):
            block = pl.ds(h * BLOCK, BLOCK)
            probs = exps[j, :, block] * factors[j, :, block]
            gs = probs * (gprobs[j, :, block] - delta[:, block])
            low[1, j, :, block] = probs.astype(BF16)
            low[0, j, :, block] = gs.astype(BF16)
        return plain_dot(low[0, j], qd[0]) * SCALE, plain_dot(low[1, j], qd[1])

    for j in range(PICKS):
        for kind, part in enumerate(backward(j)):
            terms[j, :, kind] = part.astype(BF16).reshape(CLASSES, PIECE, HEAD)
        for n in range(CLASSES):
            dz, dy = ROWS_Z - served[n // ROWS_Y], ROWS_Y - n % ROWS_Y
            holder = chip_at(dz, dy)
            src = terms.at[j, lax.rem(holder, CLASSES)]
            put(src, landed.at[j, n], BACK2 + j, holder * 2 + core, n == 3 * ROWS_Y)
        expect(BACK2 + j, landed.at[j], terms.at[0, pl.ds(0, CLASSES - 1)])
    for kind, part in enumerate(backward(PICKS)):
        own_terms[kind] = part

    for d, way in ((1, 2), (3, 0)):
        x_from = lax.rem(x + ROWS_X - d, ROWS_X)
        x_far = lax.rem(x + 2, ROWS_X)
        half = pl.ds(0, 2) if d == 1 else pl.ds(2, 2)
        arrived(ALONG_X + d)
        passed = acts.at[x_from, core, half]
        remote(passed, passed, ALONG_X + way, c, lax.rem(x + d, ROWS_X)).start()
        expect(ALONG_X + way, acts.at[x_far, core, half], acts.at[0, 0, pl.ds(0, 2)])
        across(d)

    for j in range(PICKS):
        arrived(BACK2 + j)
        both = [landed[j, :, kind].reshape(TERMS, HEAD) for kind in range(2)]
        part = plain_dot(member[j], jnp.concatenate(both, axis=1))
        if j == 0:
            totals[...] = part
        elif j < PICKS - 1:
            totals[...] += part
        else:
            part = (totals[...] + part).astype(BF16)
            for kind in range(2):
                strip = part[:, kind * HEAD : (kind + 1) * HEAD]
                sums[:, kind] = strip.reshape(CHIPS, PIECE, HEAD)

    group = z % CHUNKS
    for dz in (4, 0, 3, 7, 1, 5, 2, 6):
        for dy in (2, 1, 3, 0):
            target = chip_at(dz, dy)
            here = dz == 0 and dy == 0
            put(sums.at[target], final.at[chip], BACK1 + group, target * 2 + core, here)
    leaving.append((BACK1 + group, sums.at[pl.ds(0, CHIPS - 1)]))
    todo.extend(range(4))

    for h in range(HEADS):
        gs = low[0, :, :, pl.ds(h * BLOCK, BLOCK)].reshape((PICKS + 1) * HALF, BLOCK)
        dq = plain_dot(key_t[...], gs)
        at = pl.ds(h * HALF, HALF)
        first, second = dq[:, :HALF], dq[:, HALF:]
        dq_mine[:, at] = jnp.where(core == 0, first, second)
        dq_give[:, at] = jnp.where(core == 0, second, first)
    remote(dq_give, dq_got, DQ_PART, sibling).start()
    expect(DQ_PART, dq_got, dq_give)
    arrived(DQ_PART)
    for h in range(HEADS):
        at = pl.ds(h * HALF, HALF)
        dq = (dq_mine[:, at] + dq_got[:, at]) * SCALE
        dq_rows[:, pl.ds(h * HEAD, HEAD)] = dq.T.astype(BF16)
    local(dq_rows, dq_out, DQ).start()
    expect(DQ, dq_out)

    def collect(step):
        g, rows = chunk_of(step)
        take(final.at[pl.ds(0, 2 * ROWS_Y)], BACK1 + g)
        todo.remove(step)
        near = final[pl.ds(g * ROWS_Y, ROWS_Y)].astype(F32)
        far = final[pl.ds(CLASSES + g * ROWS_Y, ROWS_Y)].astype(F32)
        both = near + far
        for kind in range(2):
            whole = both[:, kind].reshape(CHUNK, HEAD) + own_terms[kind, rows, :]
            grads[kind, rows, :] = whole.astype(BF16)
        dst = all_grads.at[core, y, rows]
        for d in (2, 1, 3, 0):
            to = chip_at(0, d) * 2
            for swap in range(2):
                kind = core if swap == 0 else other
                put(grads.at[kind, rows], dst, GATHER + step, to + kind, d == 0 and swap == 0)
        expect(GATHER + step, all_grads.at[:, :, rows], held.at[pl.ds(0, 7 * CHUNK // (2 * PIECE))])

    def project(step):
        g, rows = chunk_of(step)
        arrived(GATHER + step)
        grads_t[...] = all_grads[:, :, rows, :].reshape(2 * ROWS_Y * CHUNK, HEAD).T
        for o in (2, 1, 3, 0):
            a = lax.rem(z // 2 + o, ROWS_X)
            features = acts[a, :, :, rows, :].reshape(2 * ROWS_Y * CHUNK, 2 * HEAD)
            part = plain_dot(grads_t[...], features)
            if step == 0:
                wide[a] = part
                continue
            if step < CHUNKS - 1:
                wide[a] += part
                continue
            part = part + wide[a]
            for s in range(2):
                z_to = 2 * a + s
                w_send[z_to] = part[:, s * HEAD : (s + 1) * HEAD].T.astype(BF16)
                for h in range(2):
                    src = w_send.at[z_to, pl.ds(h * (HEAD // 2), HEAD // 2)]
                    to = (z_to * ROWS_Y + y) * 2 + h
                    dst = wide_in.at[core, z]

                    @pl.when(to != c)
                    def _(src=src, dst=dst, to=to):
                        remote(src, dst, SUMS, to).start()

                    @pl.when(to == c)
                    def _(src=src, dst=dst):
                        local(src, dst, SUMS).start()

    collect(0)
    collect(1)
    collect(2)
    collect(3)
    local(grads, dkv_out, DKV).start()
    expect(DKV, dkv_out)
    arrived(ALONG_X)
    arrived(ALONG_X + 2)
    across(2)
    for d in range(ROWS_X):
        arrived(ACROSS + d)
    for step in range(CHUNKS - 1):
        project(step)
    project(3)
    expect(SUMS, wide_in, held.at[pl.ds(0, (2 * ROWS_Z - 1) * HEAD // (4 * PIECE))])
    arrived(SUMS)
    for kind in range(2):
        acc = wide_in[kind, 0].astype(F32)
        for d in range(1, ROWS_Z):
            acc = acc + wide_in[kind, d].astype(F32)
        dw_out[kind] = acc
    finish()


def copy_kernel(dq, dkv, dw, dq_out, dk_out, dv_out, dwk_out, dwv_out, sems):
    pairs = (
        (dq, dq_out),
        (dkv.at[0], dk_out),
        (dkv.at[1], dv_out),
        (dw.at[0], dwk_out),
        (dw.at[1], dwv_out),
    )
    copies = [pltpu.make_async_copy(src, dst, sems.at[n]) for n, (src, dst) in enumerate(pairs)]
    for one in copies:
        one.start()
    for one in copies:
        one.wait()


def body(activations, queries, key_tensor, value_tensor, output_gradient, selection, block_order):
    vmem = pl.BlockSpec(memory_space=pltpu.VMEM)
    hbm = pl.BlockSpec(memory_space=pltpu.HBM)
    dq, dkv, dw = pl.pallas_call(
        kernel,
        out_shape=(
            jax.ShapeDtypeStruct((HALF, HEADS * HEAD), BF16),
            jax.ShapeDtypeStruct((2, HALF, HEAD), BF16),
            jax.ShapeDtypeStruct((2, HEAD // 2, HEAD), F32),
        ),
        in_specs=[hbm] * 7,
        out_specs=[hbm, hbm, vmem],
        scratch_shapes=[
            pltpu.VMEM((2, QUERIES, HEAD), BF16),
            pltpu.VMEM((CLASSES, 2, PIECE, HEAD), BF16),
            pltpu.VMEM((CHIPS, 2, PIECE, HEAD), BF16),
            pltpu.VMEM((PICKS, CLASSES, 2, PIECE, HEAD), BF16),
            pltpu.VMEM((PICKS, CLASSES, 2, PIECE, HEAD), BF16),
            pltpu.VMEM((HEAD, (PICKS + 1) * HALF), BF16),
            pltpu.VMEM((PICKS + 1, HALF, QUERIES), F32),
            pltpu.VMEM((PICKS + 1, HALF, QUERIES), F32),
            pltpu.VMEM((PICKS + 1, 3, 1, QUERIES), F32),
            pltpu.VMEM((8, QUERIES), F32),
            pltpu.VMEM((8, QUERIES), F32),
            pltpu.VMEM((PICKS + 1, 1, QUERIES), F32),
            pltpu.VMEM((1, QUERIES), F32),
            pltpu.VMEM((2, PICKS + 1, HALF, QUERIES), BF16),
            pltpu.VMEM((PICKS, CLASSES, 2, PIECE, HEAD), BF16),
            pltpu.VMEM((PICKS, CLASSES, 2, PIECE, HEAD), BF16),
            pltpu.VMEM((PICKS, CHIPS * PIECE, TERMS), BF16),
            pltpu.VMEM((CHIPS * PIECE, 2 * HEAD), F32),
            pltpu.VMEM((CHIPS, 2, PIECE, HEAD), BF16),
            pltpu.VMEM((CHIPS, 2, PIECE, HEAD), BF16),
            pltpu.VMEM((2, HALF, HEAD), F32),
            pltpu.VMEM((HEAD, HEADS * HALF), F32),
            pltpu.VMEM((HEAD, HEADS * HALF), F32),
            pltpu.VMEM((HEAD, HEADS * HALF), F32),
            pltpu.VMEM((HALF, HEADS * HEAD), BF16),
            pltpu.VMEM((2, HALF, HEAD), BF16),
            pltpu.VMEM((2, ROWS_Y, HALF, HEAD), BF16),
            pltpu.VMEM((HEAD, 2 * ROWS_Y * CHUNK), BF16),
            pltpu.VMEM((ROWS_X, 2, ROWS_Y, HALF, 2 * HEAD), BF16),
            pltpu.VMEM((ROWS_X, HEAD, 2 * HEAD), F32),
            pltpu.VMEM((ROWS_Z, HEAD, HEAD), BF16),
            pltpu.VMEM((2, ROWS_Z, HEAD // 2, HEAD), BF16),
            pltpu.SMEM((PICKS, CHIPS), jnp.int32),
            pltpu.SMEM((CHIPS,), jnp.int32),
            pltpu.SMEM((CHIPS,), jnp.int32),
            pltpu.SMEM((CHIPS, PICKS), jnp.int32),
            pltpu.SemaphoreType.DMA((SEMS,)),
            pltpu.SemaphoreType.DMA((SEMS,)),
        ],
        compiler_params=pltpu.CompilerParams(
            collective_id=0, has_side_effects=True, vmem_limit_bytes=56 * 1024 * 1024
        ),
        name="attention_backward",
    )(
        activations,
        queries,
        key_tensor.reshape(CLASSES, PIECE, HEAD),
        value_tensor.reshape(CLASSES, PIECE, HEAD),
        output_gradient,
        selection.T,
        block_order,
    )
    shapes = (dq.shape, dkv.shape[1:], dkv.shape[1:], dw.shape[1:], dw.shape[1:])
    kinds = (BF16, BF16, BF16, F32, F32)
    return pl.pallas_call(
        copy_kernel,
        out_shape=tuple(jax.ShapeDtypeStruct(s, t) for s, t in zip(shapes, kinds)),
        in_specs=[hbm] * 3,
        out_specs=[vmem] * 5,
        scratch_shapes=[pltpu.SemaphoreType.DMA((5,))],
        name="copy_out",
    )(dq, dkv, dw)


def solution(mesh):
    placed = (P("ctx", "tp"),) * 5 + (P(), P())
    return jax.shard_map(
        body,
        mesh=mesh,
        in_specs=placed,
        out_specs=(P("ctx", "tp"),) * 5,
        check_vma=False,
    )
```

```python
import functools
import math

import jax
import jax.numpy as jnp
from jax import lax
from jax.experimental import pallas as pl
from jax.experimental.pallas import tpu as pltpu
from jax.sharding import PartitionSpec as P

MESH = pl.DeviceIdType.MESH
F32 = jnp.float32
BF16 = jnp.bfloat16

HEAD = 128
BLOCK = 512
HALF = 256
PICKS = 3
CHIPS = 32
ROWS_Y = 4
ROWS_Z = 8
ROWS_X = 4
CLASSES = 16
REPLICAS = 2
PIECE = HALF // CLASSES
CHUNKS = 4
CHUNK = HALF // CHUNKS
TERMS = CLASSES * PIECE
HEADS = 4
QUERIES = HEADS * BLOCK
SCALE = HEAD**-0.5
EXP_SCALE = SCALE * math.log2(math.e)
LOW = -1e30

(LOAD, P1, PACK, ACT1, STATS, SUMS, LISTS, ORDER, DQ, DQ_PART, DKV) = range(11)
P2 = 11
ALONG_X = P2 + PICKS
BACK2 = ALONG_X + ROWS_X
BACK1 = BACK2 + PICKS
GATHER = BACK1 + CHUNKS
ACROSS = GATHER + CHUNKS
SEMS = ACROSS + ROWS_X


def rows_dot(left, right):
    return lax.dot_general(left, right, (((1,), (1,)), ((), ())), preferred_element_type=F32)


def plain_dot(left, right):
    return lax.dot_general(left, right, (((1,), (0,)), ((), ())), preferred_element_type=F32)


def kernel(
    act_in,
    q_in,
    k_in,
    v_in,
    go_in,
    selection_in,
    order_in,
    dq_out,
    dkv_out,
    dw_out,
    qd,
    packed,
    held,
    picked,
    kv,
    key_t,
    exps,
    gprobs,
    stats,
    my_stats,
    their_stats,
    factors,
    delta,
    low,
    terms,
    landed,
    member,
    totals,
    sums,
    final,
    own_terms,
    dq_mine,
    dq_give,
    dq_got,
    dq_rows,
    grads,
    all_grads,
    grads_t,
    acts,
    wide,
    w_send,
    wide_in,
    selection,
    order,
    inverse,
    table,
    send,
    recv,
):
    c = lax.axis_index("ctx")
    x = lax.axis_index("tp")
    chip = c // 2
    core = c % 2
    z = chip // ROWS_Y
    y = chip % ROWS_Y
    other = 1 - core
    sibling = c + 1 - 2 * core
    piece_class = chip % CLASSES
    served = (2 + 4 * core, ROWS_Z - 1, 1, 0)

    def chip_at(dz, dy):
        return lax.rem(z + dz, ROWS_Z) * ROWS_Y + lax.rem(y + dy, ROWS_Y)

    def remote(src, dst, sem, ctx, tp=None):
        return pltpu.make_async_remote_copy(
            src_ref=src,
            dst_ref=dst,
            send_sem=send.at[sem],
            recv_sem=recv.at[sem],
            device_id=(ctx, x if tp is None else tp),
            device_id_type=MESH,
        )

    def local(src, dst, sem):
        return pltpu.make_async_copy(src, dst, recv.at[sem])

    def put(src, dst, sem, ctx, here):
        if here:
            local(src, dst, sem).start()
        else:
            remote(src, dst, sem, ctx).start()

    coming = {}
    leaving = []

    def expect(sem, arrives, leaves=None):
        coming[sem] = arrives
        if leaves is not None:
            leaving.append((sem, leaves))

    def take(ref, sem):
        pltpu.make_async_copy(ref, ref, recv.at[sem]).wait()

    def arrived(sem):
        take(coming.pop(sem), sem)

    def sent(ref, sem):
        pltpu.make_async_copy(ref, ref, send.at[sem]).wait()

    todo = []

    def finish():
        for st in todo:
            g, rows = chunk_of(st)
            take(final.at[pl.ds(0, 2 * ROWS_Y)], BACK1 + g)
        for sem in list(coming):
            arrived(sem)
        for sem, ref in leaving:
            sent(ref, sem)
        leaving.clear()

    def chunk_of(step):
        g = lax.rem(z + (0, 1, 3, 2)[step], CHUNKS)
        return g, pl.ds(pl.multiple_of(g * CHUNK, CHUNK), CHUNK)

    barrier = pltpu.get_barrier_semaphore()

    def hello(ctx, tp=None):
        pl.semaphore_signal(
            barrier, inc=1, device_id=(ctx, x if tp is None else tp), device_id_type=MESH
        )

    far_first = (4, 3, 5, 2, 6, 1, 7, 0)
    peers = 0
    for dz in far_first:
        for dy in (2, 1, 3, 0):
            if dz or dy:
                hello(chip_at(dz, dy) * 2 + core)
                peers += 1
            if dz == 0 or dy == 0:
                hello(chip_at(dz, dy) * 2 + other)
                peers += 1
    for d in range(1, ROWS_X):
        hello(c, lax.rem(x + d, ROWS_X))
        peers += 1

    local(selection_in, selection, LISTS).start()
    local(order_in, order, ORDER).start()
    expect(LISTS, selection)
    expect(ORDER, order)
    for kind, src in ((0, k_in), (1, v_in)):
        local(src, packed.at[:, kind], PACK).start()
    expect(PACK, packed)
    arrived(PACK)

    pl.semaphore_wait(barrier, peers)

    for dz in far_first:
        for dy in (2, 1, 3, 0):
            target = chip_at(dz, dy)
            src = packed.at[lax.rem(target, CLASSES)]
            put(src, held.at[chip], P1, target * 2 + core, dz == 0 and dy == 0)
    expect(P1, held, held.at[pl.ds(0, CHIPS - 1)])

    for d in range(ROWS_Y):
        y_to = lax.rem(y + d, ROWS_Y)
        for s in range(2):
            src = act_in.at[:, pl.ds(pl.multiple_of((y_to + ROWS_Y * s) * HEAD, HEAD), HEAD)]
            dst = acts.at[x, core, y, :, pl.ds(s * HEAD, HEAD)]
            put(src, dst, ACT1, (z * ROWS_Y + y_to) * 2 + core, d == 0)
    expect(ACT1, acts.at[x, core], acts.at[0, 0, pl.ds(0, ROWS_Y - 1)])

    for h in range(HEADS):
        strip = pl.ds(h * HEAD, HEAD)
        rows = pl.ds(pl.multiple_of(h * BLOCK + core * HALF, HALF), HALF)
        for kind, src in ((0, q_in), (1, go_in)):
            remote(src.at[:, strip], qd.at[kind, rows], LOAD, sibling).start()
            local(src.at[:, strip], qd.at[kind, rows], LOAD).start()
    expect(LOAD, qd, qd.at[0])

    arrived(ORDER)
    arrived(LISTS)

    def invert(e, carry):
        at = jnp.int32(0)
        for b in range(CHIPS):
            at = jnp.where(order[b] == e, b, at)
        inverse[e] = at
        return carry

    lax.fori_loop(0, CHIPS, invert, 0)

    def look_up(t, carry):
        for j in range(PICKS):
            table[t, j] = inverse[selection[j, order[t]]]
        return carry

    lax.fori_loop(0, CHIPS, look_up, 0)
    def lines(kind, j):
        source = packed if j == PICKS else kv.at[j]
        return source[:, kind].reshape(HALF, HEAD)

    def forward(j):
        keys = lines(0, j)
        values = lines(1, j)
        key_t[:, pl.ds(j * HALF, HALF)] = keys.T
        for h in range(HEADS):
            block = pl.ds(h * BLOCK, BLOCK)
            raw = rows_dot(keys, qd[0, block, :])
            if j == PICKS:
                key_at = lax.broadcasted_iota(jnp.int32, raw.shape, 0) + core * HALF
                query_at = lax.broadcasted_iota(jnp.int32, raw.shape, 1)
                raw = jnp.where(key_at <= query_at, raw, LOW)
            top = jnp.max(raw, axis=0, keepdims=True)
            weights = jnp.exp2((raw - top) * EXP_SCALE)
            gp = rows_dot(values, qd[1, block, :])
            exps[j, :, block] = weights
            gprobs[j, :, block] = gp
            stats[j, 0, pl.ds(h, 1), :] = top
            stats[j, 1, pl.ds(h, 1), :] = jnp.sum(weights, axis=0, keepdims=True)
            stats[j, 2, pl.ds(h, 1), :] = jnp.sum(weights * gp, axis=0, keepdims=True)


    arrived(P1)

    for j in range(PICKS):
        for n in range(CLASSES):
            dz, dy = served[n // ROWS_Y], n % ROWS_Y
            target = chip_at(dz, dy)
            picked[j, n] = held[table[target, j]]
            dst = kv.at[j, piece_class]
            put(picked.at[j, n], dst, P2 + j, target * 2 + core, n == 3 * ROWS_Y)
        expect(P2 + j, kv.at[j], kv.at[0, pl.ds(0, CLASSES - 1)])

    def across(d):
        x_from = lax.rem(x + ROWS_X - d, ROWS_X)
        remote(acts.at[x_from, core], acts.at[x_from, core], ACROSS + d, sibling).start()
        expect(ACROSS + d, acts.at[x_from, other], acts.at[0, 0])

    arrived(ACT1)
    for d in (1, 3):
        x_to = lax.rem(x + d, ROWS_X)
        remote(acts.at[x, core], acts.at[x, core], ALONG_X + d, c, x_to).start()
        x_from = lax.rem(x + ROWS_X - d, ROWS_X)
        expect(ALONG_X + d, acts.at[x_from, core], acts.at[0, 0])
    across(0)
    arrived(LOAD)
    forward(PICKS)

    column = lax.broadcasted_iota(jnp.int32, (1, TERMS), 1)
    step_rows = 4 * PIECE
    row = lax.broadcasted_iota(jnp.int32, (step_rows, TERMS), 0)
    same = jnp.where(
        row % PIECE == lax.broadcasted_iota(jnp.int32, (step_rows, TERMS), 1) % PIECE, 1.0, 0.0
    )
    for j in range(PICKS):
        wanted = jnp.zeros((1, TERMS), jnp.int32)
        for n in range(CLASSES):
            client = chip_at(served[n // ROWS_Y], n % ROWS_Y)
            wanted = jnp.where(column // PIECE == n, table[client, j], wanted)

        def fill(r, carry, j=j, wanted=wanted):
            hit = row // PIECE + 4 * r == wanted
            at = pl.ds(pl.multiple_of(r * step_rows, step_rows), step_rows)
            member[j, at, :] = jnp.where(hit, same, 0.0).astype(BF16)
            return carry

        lax.fori_loop(0, CHIPS // 4, fill, 0)


    arrived(P2)
    forward(0)
    arrived(P2 + 1)
    forward(1)
    arrived(P2+2)
    forward(2)

    mine_at = order[chip]
    alive = [selection[j, mine_at] != mine_at for j in range(PICKS)] + [True]

    def part_of(top, peak):
        return jnp.exp2(jnp.minimum(top - peak, 0.0) * EXP_SCALE)

    peak = stats[PICKS, 0]
    for j in range(PICKS):
        peak = jnp.maximum(peak, jnp.where(alive[j], stats[j, 0], LOW))
    total = jnp.zeros((HEADS, BLOCK), F32)
    turned = jnp.zeros((HEADS, BLOCK), F32)
    parts = []
    for j in range(PICKS + 1):
        part = jnp.where(alive[j], part_of(stats[j, 0], peak), 0.0)
        parts.append(part)
        total = total + part * stats[j, 1]
        turned = turned + part * stats[j, 2]
    my_stats[0] = peak
    my_stats[1] = total
    my_stats[2] = turned
    remote(my_stats, their_stats, STATS, sibling).start()
    expect(STATS, their_stats, my_stats)
    arrived(STATS)
    their_peak = their_stats[0]
    top = jnp.maximum(peak, their_peak)
    mine_part = part_of(peak, top)
    their_part = part_of(their_peak, top)
    share = 1.0 / (mine_part * total + their_part * their_stats[1])
    delta[...] = (mine_part * turned + their_part * their_stats[2]) * share
    for j in range(PICKS + 1):
        factors[j] = parts[j] * (mine_part * share)

    def backward(j):
        for h in range(HEADS):
            block = pl.ds(h * BLOCK, BLOCK)
            probs = exps[j, :, block] * factors[j, pl.ds(h, 1), :]
            gs = probs * (gprobs[j, :, block] - delta[pl.ds(h, 1), :])
            low[1, j, :, block] = probs.astype(BF16)
            low[0, j, :, block] = gs.astype(BF16)
        return plain_dot(low[0, j], qd[0]) * SCALE, plain_dot(low[1, j], qd[1])

    for j in range(PICKS):
        for kind, part in enumerate(backward(j)):
            terms[j, :, kind] = part.astype(BF16).reshape(CLASSES, PIECE, HEAD)
        for n in range(CLASSES):
            dz, dy = ROWS_Z - served[n // ROWS_Y], ROWS_Y - n % ROWS_Y
            holder = chip_at(dz, dy)
            src = terms.at[j, lax.rem(holder, CLASSES)]
            put(src, landed.at[j, n], BACK2 + j, holder * 2 + core, n == 3 * ROWS_Y)
        expect(BACK2 + j, landed.at[j], terms.at[0, pl.ds(0, CLASSES - 1)])
    for kind, part in enumerate(backward(PICKS)):
        own_terms[kind] = part

    for d, way in ((1, 2), (3, 0)):
        x_from = lax.rem(x + ROWS_X - d, ROWS_X)
        x_far = lax.rem(x + 2, ROWS_X)
        half = pl.ds(0, 2) if d == 1 else pl.ds(2, 2)
        arrived(ALONG_X + d)
        passed = acts.at[x_from, core, half]
        remote(passed, passed, ALONG_X + way, c, lax.rem(x + d, ROWS_X)).start()
        expect(ALONG_X + way, acts.at[x_far, core, half], acts.at[0, 0, pl.ds(0, 2)])
        across(d)

    for j in range(PICKS):
        arrived(BACK2 + j)
        both = [landed[j, :, kind].reshape(TERMS, HEAD) for kind in range(2)]
        part = plain_dot(member[j], jnp.concatenate(both, axis=1))
        if j == 0:
            totals[...] = part
        elif j < PICKS - 1:
            totals[...] += part
        else:
            part = (totals[...] + part).astype(BF16)
            for kind in range(2):
                strip = part[:, kind * HEAD : (kind + 1) * HEAD]
                sums[:, kind] = strip.reshape(CHIPS, PIECE, HEAD)

    group = z % CHUNKS
    for dz in (4, 0, 3, 7, 1, 5, 2, 6):
        for dy in (2, 1, 3, 0):
            target = chip_at(dz, dy)
            here = dz == 0 and dy == 0
            put(sums.at[target], final.at[chip], BACK1 + group, target * 2 + core, here)
    leaving.append((BACK1 + group, sums.at[pl.ds(0, CHIPS - 1)]))
    todo.extend(range(4))

    for h in range(HEADS):
        gs = low[0, :, :, pl.ds(h * BLOCK, BLOCK)].reshape((PICKS + 1) * HALF, BLOCK)
        dq = plain_dot(key_t[...], gs)
        at = pl.ds(h * HALF, HALF)
        first, second = dq[:, :HALF], dq[:, HALF:]
        dq_mine[:, at] = jnp.where(core == 0, first, second)
        dq_give[:, at] = jnp.where(core == 0, second, first)
    remote(dq_give, dq_got, DQ_PART, sibling).start()
    expect(DQ_PART, dq_got, dq_give)
    arrived(DQ_PART)
    for h in range(HEADS):
        at = pl.ds(h * HALF, HALF)
        dq = (dq_mine[:, at] + dq_got[:, at]) * SCALE
        dq_rows[:, pl.ds(h * HEAD, HEAD)] = dq.T.astype(BF16)
    local(dq_rows, dq_out, DQ).start()
    expect(DQ, dq_out)

    def collect(step):
        g, rows = chunk_of(step)
        take(final.at[pl.ds(0, 2 * ROWS_Y)], BACK1 + g)
        todo.remove(step)
        near = final[pl.ds(g * ROWS_Y, ROWS_Y)].astype(F32)
        far = final[pl.ds(CLASSES + g * ROWS_Y, ROWS_Y)].astype(F32)
        both = near + far
        for kind in range(2):
            whole = both[:, kind].reshape(CHUNK, HEAD) + own_terms[kind, rows, :]
            grads[kind, rows, :] = whole.astype(BF16)
        dst = all_grads.at[core, y, rows]
        for d in (2, 1, 3, 0):
            to = chip_at(0, d) * 2
            for swap in range(2):
                kind = core if swap == 0 else other
                put(grads.at[kind, rows], dst, GATHER + step, to + kind, d == 0 and swap == 0)
        expect(GATHER + step, all_grads.at[:, :, rows], held.at[pl.ds(0, 7 * CHUNK // (2 * PIECE))])

    def project(step):
        g, rows = chunk_of(step)
        arrived(GATHER + step)
        grads_t[...] = all_grads[:, :, rows, :].reshape(2 * ROWS_Y * CHUNK, HEAD).T
        for o in (2, 1, 3, 0):
            a = lax.rem(z // 2 + o, ROWS_X)
            features = acts[a, :, :, rows, :].reshape(2 * ROWS_Y * CHUNK, 2 * HEAD)
            part = plain_dot(grads_t[...], features)
            if step == 0:
                wide[a] = part
                continue
            if step < CHUNKS - 1:
                wide[a] += part
                continue
            part = part + wide[a]
            for s in range(2):
                z_to = 2 * a + s
                w_send[z_to] = part[:, s * HEAD : (s + 1) * HEAD].T.astype(BF16)
                for h in range(2):
                    src = w_send.at[z_to, pl.ds(h * (HEAD // 2), HEAD // 2)]
                    to = (z_to * ROWS_Y + y) * 2 + h
                    dst = wide_in.at[core, z]

                    @pl.when(to != c)
                    def _(src=src, dst=dst, to=to):
                        remote(src, dst, SUMS, to).start()

                    @pl.when(to == c)
                    def _(src=src, dst=dst):
                        local(src, dst, SUMS).start()

    collect(0)
    collect(1)
    collect(2)
    collect(3)
    local(grads, dkv_out, DKV).start()
    expect(DKV, dkv_out)
    arrived(ALONG_X)
    arrived(ALONG_X + 2)
    across(2)
    for d in range(ROWS_X):
        arrived(ACROSS + d)
    for step in range(CHUNKS - 1):
        project(step)
    project(3)
    finish()
    expect(SUMS, wide_in, held.at[pl.ds(0, (2 * ROWS_Z - 1) * HEAD // (4 * PIECE))])
    arrived(SUMS)
    for kind in range(2):
        acc = wide_in[kind, 0].astype(F32)
        for d in range(1, ROWS_Z):
            acc = acc + wide_in[kind, d].astype(F32)
        dw_out[kind] = acc
    finish()


def copy_kernel(dq, dkv, dw, dq_out, dk_out, dv_out, dwk_out, dwv_out, sems):
    pairs = (
        (dq, dq_out),
        (dkv.at[0], dk_out),
        (dkv.at[1], dv_out),
        (dw.at[0], dwk_out),
        (dw.at[1], dwv_out),
    )
    copies = [pltpu.make_async_copy(src, dst, sems.at[n]) for n, (src, dst) in enumerate(pairs)]
    for one in copies:
        one.start()
    for one in copies:
        one.wait()


def body(activations, queries, key_tensor, value_tensor, output_gradient, selection, block_order):
    vmem = pl.BlockSpec(memory_space=pltpu.VMEM)
    hbm = pl.BlockSpec(memory_space=pltpu.HBM)
    dq, dkv, dw = pl.pallas_call(
        kernel,
        out_shape=(
            jax.ShapeDtypeStruct((HALF, HEADS * HEAD), BF16),
            jax.ShapeDtypeStruct((2, HALF, HEAD), BF16),
            jax.ShapeDtypeStruct((2, HEAD // 2, HEAD), F32),
        ),
        in_specs=[hbm] * 7,
        out_specs=[hbm, hbm, vmem],
        scratch_shapes=[
            pltpu.VMEM((2, QUERIES, HEAD), BF16),
            pltpu.VMEM((CLASSES, 2, PIECE, HEAD), BF16),
            pltpu.VMEM((CHIPS, 2, PIECE, HEAD), BF16),
            pltpu.VMEM((PICKS, CLASSES, 2, PIECE, HEAD), BF16),
            pltpu.VMEM((PICKS, CLASSES, 2, PIECE, HEAD), BF16),
            pltpu.VMEM((HEAD, (PICKS + 1) * HALF), BF16),
            pltpu.VMEM((PICKS + 1, HALF, QUERIES), F32),
            pltpu.VMEM((PICKS + 1, HALF, QUERIES), F32),
            pltpu.VMEM((PICKS + 1, 3, HEADS, BLOCK), F32),
            pltpu.VMEM((3, HEADS, BLOCK), F32),
            pltpu.VMEM((3, HEADS, BLOCK), F32),
            pltpu.VMEM((PICKS + 1, HEADS, BLOCK), F32),
            pltpu.VMEM((HEADS, BLOCK), F32),
            pltpu.VMEM((2, PICKS + 1, HALF, QUERIES), BF16),
            pltpu.VMEM((PICKS, CLASSES, 2, PIECE, HEAD), BF16),
            pltpu.VMEM((PICKS, CLASSES, 2, PIECE, HEAD), BF16),
            pltpu.VMEM((PICKS, CHIPS * PIECE, TERMS), BF16),
            pltpu.VMEM((CHIPS * PIECE, 2 * HEAD), F32),
            pltpu.VMEM((CHIPS, 2, PIECE, HEAD), BF16),
            pltpu.VMEM((CHIPS, 2, PIECE, HEAD), BF16),
            pltpu.VMEM((2, HALF, HEAD), F32),
            pltpu.VMEM((HEAD, HEADS * HALF), F32),
            pltpu.VMEM((HEAD, HEADS * HALF), F32),
            pltpu.VMEM((HEAD, HEADS * HALF), F32),
            pltpu.VMEM((HALF, HEADS * HEAD), BF16),
            pltpu.VMEM((2, HALF, HEAD), BF16),
            pltpu.VMEM((2, ROWS_Y, HALF, HEAD), BF16),
            pltpu.VMEM((HEAD, 2 * ROWS_Y * CHUNK), BF16),
            pltpu.VMEM((ROWS_X, 2, ROWS_Y, HALF, 2 * HEAD), BF16),
            pltpu.VMEM((ROWS_X, HEAD, 2 * HEAD), F32),
            pltpu.VMEM((ROWS_Z, HEAD, HEAD), BF16),
            pltpu.VMEM((2, ROWS_Z, HEAD // 2, HEAD), BF16),
            pltpu.SMEM((PICKS, CHIPS), jnp.int32),
            pltpu.SMEM((CHIPS,), jnp.int32),
            pltpu.SMEM((CHIPS,), jnp.int32),
            pltpu.SMEM((CHIPS, PICKS), jnp.int32),
            pltpu.SemaphoreType.DMA((SEMS,)),
            pltpu.SemaphoreType.DMA((SEMS,)),
        ],
        compiler_params=pltpu.CompilerParams(
            collective_id=0, has_side_effects=True, vmem_limit_bytes=56 * 1024 * 1024
        ),
        name="attention_backward",
    )(
        activations,
        queries,
        key_tensor.reshape(CLASSES, PIECE, HEAD),
        value_tensor.reshape(CLASSES, PIECE, HEAD),
        output_gradient,
        selection.T,
        block_order,
    )
    shapes = (dq.shape, dkv.shape[1:], dkv.shape[1:], dw.shape[1:], dw.shape[1:])
    kinds = (BF16, BF16, BF16, F32, F32)
    return pl.pallas_call(
        copy_kernel,
        out_shape=tuple(jax.ShapeDtypeStruct(s, t) for s, t in zip(shapes, kinds)),
        in_specs=[hbm] * 3,
        out_specs=[vmem] * 5,
        scratch_shapes=[pltpu.SemaphoreType.DMA((5,))],
        name="copy_out",
    )(dq, dkv, dw)


def solution(mesh):
    placed = (P("ctx", "tp"),) * 5 + (P(), P())
    return jax.shard_map(
        body,
        mesh=mesh,
        in_specs=placed,
        out_specs=(P("ctx", "tp"),) * 5,
        check_vma=False,
    )
```
